32 devices in a mesh: seq: 8 (over z, core), tensor: 4 (over y, x).
Axes of the slice: x: 2, y: 2, z: 4, core: 2. Of those that a mesh axis runs over, the one named last changes fastest.
Arguments:
- tokens: bfloat16 [2, 1024, 3072], P(None, ('seq', 'tensor')), may hold values from -6 to 6
- qkv_weight: bfloat16 [48, 192, 3072], P('tensor'), may hold values from -0.109375 to 0.109375
- rate_weight: bfloat16 [48, 3072], P('tensor'), may hold values from -0.109375 to 0.109375
- base_rate: float32 [48], P('tensor'), may hold values from 0.003 to 0.03
- first_w: float32 [48, 64, 256], P('tensor'), may hold values from -0.75 to 0.75
- first_b: float32 [48, 256], P('tensor'), may hold values from -3 to 3
- second_w: float32 [48, 256, 64], P('tensor'), may hold values from -0.375 to 0.375
- second_b: float32 [48, 64], P('tensor'), may hold values from -3 to 3
- norm_gain: float32 [48, 64], P('tensor'), may hold values from 0.5 to 1.5
- norm_shift: float32 [48, 64], P('tensor'), may hold values from -3 to 3
- out_weight: bfloat16 [3072, 3072], P('tensor'), may hold values from -0.109375 to 0.109375
Outputs:
- mixed: bfloat16 [2, 1024, 3072], P(None, ('seq', 'tensor'))
The draws below stay inside these ranges and needn't reach their ends.
All inputs are finite; a program needn't handle non-finite values.
Results may differ from the reference program's by a relative error of at most 0.019.
Values may be sent and summed in bfloat16 or wider, within the bound.
A program may use at most 64 MiB of HBM per device.

```python
import math
import jax
import jax.numpy as jnp
from jax import lax

D = 3072
HEADS = 48
HEAD = 64
INNER = 256
MB = 64
SEQS = 2
LENGTH = 1024


def block_scale(rng, extent, cuts, least, top_value):
    level = 1.0
    for position, shards_of in cuts:
        steps = jax.random.uniform(jax.random.fold_in(jax.random.fold_in(rng, 6), position), (shards_of,), jnp.float32, least / len(cuts), top_value / len(cuts))
        level = level * jnp.repeat(jnp.exp(steps), extent[position] // shards_of).reshape((-1,) + (1,) * (len(extent) - 1 - position))
    return level


def gaussian(rng, dims, spread, limit, pieces=(), dtype=jnp.bfloat16):
    gain = block_scale(rng, dims, pieces, -0.22, 0.18) if pieces else 1.0
    values = jax.random.normal(rng, dims, jnp.float32) * spread * gain
    return jnp.minimum(jnp.maximum(values, -limit), limit).astype(dtype)


def setup_inputs(seed: int = 0) -> dict:
    seeds = jax.random.split(jax.random.key(seed), 12)
    tokens = gaussian(seeds[0], (SEQS, LENGTH, D), 1.0, 6.0, ((1, 32),))
    qkv_weight = gaussian(seeds[1], (HEADS, 3 * HEAD, D), D ** -0.5, 0.109375, ((0, 4),))
    rate_weight = gaussian(seeds[2], (HEADS, D), D ** -0.5, 0.109375, ((0, 4),))
    base_rate = jnp.clip(jnp.exp(math.log(0.03) - 2.3025851 * jax.random.uniform(seeds[3], (HEADS,), jnp.float32) ** block_scale(seeds[3], (HEADS,), ((0, 4),), -0.2, 0.2)), 0.003, 0.03)
    first_w = gaussian(seeds[4], (HEADS, HEAD, INNER), HEAD ** -0.5, 0.75, ((0, 4),), jnp.float32)
    first_b = gaussian(seeds[5], (HEADS, INNER), 0.5, 3.0, ((0, 4),), jnp.float32)
    second_w = gaussian(seeds[6], (HEADS, INNER, HEAD), INNER ** -0.5, 0.375, ((0, 4),), jnp.float32)
    second_b = gaussian(seeds[7], (HEADS, HEAD), 0.5, 3.0, ((0, 4),), jnp.float32)
    norm_gain = jnp.clip(1.0 + 0.1 * jax.random.normal(seeds[8], (HEADS, HEAD), jnp.float32), 0.5, 1.5)
    norm_shift = gaussian(seeds[9], (HEADS, HEAD), 0.5, 3.0, ((0, 4),), jnp.float32)
    out_weight = gaussian(seeds[10], (HEADS * HEAD, D), (HEADS * HEAD) ** -0.5, 0.109375, ((0, 4),))
    return {"tokens": tokens, "qkv_weight": qkv_weight, "rate_weight": rate_weight, "base_rate": base_rate, "first_w": first_w, "first_b": first_b, "second_w": second_w, "second_b": second_b, "norm_gain": norm_gain, "norm_shift": norm_shift, "out_weight": out_weight}


def smooth_gate(values):
    return jax.nn.gelu(values, approximate=True)

def apply_model(rows, weights, norm_gain, norm_shift):
    first_w, first_b, second_w, second_b = weights
    pre_act = jnp.dot(rows, first_w.astype(jnp.bfloat16), preferred_element_type=jnp.float32) + first_b
    hidden = smooth_gate(pre_act).astype(jnp.bfloat16)
    outer = jnp.dot(hidden, second_w.astype(jnp.bfloat16), preferred_element_type=jnp.float32) + second_b
    average = lax.optimization_barrier(jnp.mean(outer, axis=-1, keepdims=True))
    centered = outer - average
    inverse = lax.rsqrt(lax.optimization_barrier(jnp.mean(centered * centered, axis=-1, keepdims=True)) + 1e-06)
    normed = centered * inverse
    return (pre_act, hidden, normed, inverse, norm_gain * normed + norm_shift)

def block_update(weights, block, norm_gain, norm_shift):
    queries, key_rows, value_rows, rates = block
    first_w, first_b, second_w, second_b = weights
    pre_act, hidden, normed, inverse, predicted = apply_model(key_rows, weights, norm_gain, norm_shift)
    target = value_rows.astype(jnp.float32) - key_rows.astype(jnp.float32)
    upstream = (predicted - target) * norm_gain
    grad_outer = inverse * (upstream - lax.optimization_barrier(jnp.mean(upstream, axis=-1, keepdims=True)) - normed * lax.optimization_barrier(jnp.mean(upstream * normed, axis=-1, keepdims=True)))
    weighted_outer = rates[:, None] * grad_outer
    scaled_outer = weighted_outer.astype(jnp.bfloat16)
    plain_outer = grad_outer.astype(jnp.bfloat16)
    grad_hidden = jnp.dot(plain_outer, second_w.astype(jnp.bfloat16).T, preferred_element_type=jnp.float32)
    unused, pullback = jax.vjp(smooth_gate, pre_act)
    grad_inner = pullback(grad_hidden)[0]
    weighted_inner = rates[:, None] * grad_inner
    scaled_inner = weighted_inner.astype(jnp.bfloat16)
    new_weights = (first_w - jnp.dot(key_rows.T, scaled_inner, preferred_element_type=jnp.float32), first_b - lax.optimization_barrier(jnp.sum(weighted_inner, axis=0)), second_w - jnp.dot(hidden.T, scaled_outer, preferred_element_type=jnp.float32), second_b - lax.optimization_barrier(jnp.sum(weighted_outer, axis=0)))
    answer = apply_model(queries, new_weights, norm_gain, norm_shift)[4] + queries.astype(jnp.float32)
    return (new_weights, answer.astype(jnp.bfloat16))

def head_chain(weights, queries, key_rows, value_rows, rates, norm_gain, norm_shift):
    block_count = queries.shape[0] // MB
    stacked = (queries.reshape(block_count, MB, -1), key_rows.reshape(block_count, MB, -1), value_rows.reshape(block_count, MB, -1), rates.reshape(block_count, MB))

    def advance(state, block):
        return block_update(state, block, norm_gain, norm_shift)
    final, produced = lax.scan(advance, weights, stacked)
    return (final, produced.reshape(queries.shape[0], -1))

def reference(tokens, qkv_weight, rate_weight, base_rate, first_w, first_b, second_w, second_b, norm_gain, norm_shift, out_weight):
    chains = jax.vmap(head_chain, in_axes=((0, 0, 0, 0), 1, 1, 1, 1, 0, 0), out_axes=(0, 1))

    def one_sequence(sequence):
        projected = jnp.dot(sequence, qkv_weight.reshape(HEADS * 3 * HEAD, D).T, preferred_element_type=jnp.float32)
        projected = projected.astype(jnp.bfloat16).reshape(LENGTH, HEADS, 3 * HEAD)
        queries = projected[:, :, :HEAD]
        key_rows = projected[:, :, HEAD:2 * HEAD]
        value_rows = projected[:, :, 2 * HEAD:]
        rates = base_rate * jax.nn.sigmoid(jnp.dot(sequence, rate_weight.T, preferred_element_type=jnp.float32))
        unused, head_out = chains((first_w, first_b, second_w, second_b), queries, key_rows, value_rows, rates, norm_gain, norm_shift)
        mixed = jnp.dot(head_out.reshape(LENGTH, HEADS * HEAD), out_weight, preferred_element_type=jnp.float32)
        return mixed.astype(jnp.bfloat16)
    return lax.map(one_sequence, tokens)
```

```python
import functools
import math

import jax
import jax.numpy as jnp
from jax import lax
from jax.experimental import pallas as pl
from jax.experimental.pallas import tpu as pltpu
from jax.sharding import PartitionSpec as P

HEAD = 64
MB = 64
TILE = 128
ROWS = 3 * HEAD + 16
CURVE = math.sqrt(2.0 / math.pi)
CUBIC = 0.044715
F32 = jnp.float32
BF16 = jnp.bfloat16
NN = (((1,), (0,)), ((), ()))
NT = (((1,), (1,)), ((), ()))


def dot(a, b, dims=NN):
    return lax.dot_general(a, b, dims, preferred_element_type=F32)


def split_bias(state):
    lane = lax.broadcasted_iota(jnp.int32, state.shape, 1)
    rest = state - state.astype(BF16).astype(F32)
    return jnp.where(lane == HEAD + 1, rest, state).astype(BF16)


def mean_rows(values):
    return jnp.sum(values, axis=0, keepdims=True) * (1.0 / HEAD)


def load_state(count, first, second, second_t, state):
    w1, w2, w2t, w1b, w2b, w2tb = state
    for c in range(count):
        w1[c] = first[c]
        w2[c] = second[c]
        w2t[c] = second_t[c]
        w1b[c] = split_bias(first[c])
        w2b[c] = second[c].astype(BF16)
        w2tb[c] = second_t[c].astype(BF16)


def mini_batch(count, keys_low, learn, key_tile, query_tile, consts, state, bias2):
    gain, shift = consts
    w1, w2, w2t, w1b, w2b, w2tb = state
    each = range(count)
    lane = lax.broadcasted_iota(jnp.int32, (HEAD, TILE), 1)
    is_key = (lane < MB) if keys_low else (lane >= MB)
    row = lax.broadcasted_iota(jnp.int32, (HEAD, TILE), 0)
    ones_rows = jnp.where(row < 2, 1.0, 0.0)
    rows = [
        jnp.where(
            is_key,
            key_tile[c, HEAD : 2 * HEAD, :].astype(F32),
            query_tile[c, :HEAD, :].astype(F32),
        )
        for c in each
    ]
    wide = [jnp.concatenate([rows[c], ones_rows], axis=0).astype(BF16) for c in each]
    pre = [dot(w1b[c], wide[c]) for c in each]
    square = [p * p for p in pre]
    bend = [jnp.tanh((CURVE * p) * (1.0 + CUBIC * s)) for p, s in zip(pre, square)]
    half = [0.5 + 0.5 * t for t in bend]
    hidden = [(p * h).astype(BF16) for p, h in zip(pre, half)]
    outer = [dot(w2tb[c], hidden[c]) + bias2[c] for c in each]
    centered = [o - mean_rows(o) for o in outer]
    inverse = [lax.rsqrt(mean_rows(z * z) + 1e-06) for z in centered]
    normed = [z * i for z, i in zip(centered, inverse)]
    model = [gain[c] * normed[c] + shift[c] for c in each]
    answer = [rows[c] + model[c] for c in each]
    if not learn:
        return answer
    values = [key_tile[c, 2 * HEAD : 3 * HEAD, :].astype(F32) for c in each]
    upstream = [(model[c] - (values[c] - rows[c])) * gain[c] for c in each]
    grad_outer = [
        inverse[c]
        * (
            upstream[c]
            - mean_rows(upstream[c])
            - normed[c] * mean_rows(upstream[c] * normed[c])
        )
        for c in each
    ]
    rates = []
    for c in each:
        pair = key_tile[c, 3 * HEAD : 3 * HEAD + 16, :].astype(F32)
        rate = pair[0:1, :] + pair[1:2, :]
        rates.append(jnp.where(is_key[0:1, :], rate, 0.0))
    plain = [g.astype(BF16) for g in grad_outer]
    scaled_outer = [(rates[c] * grad_outer[c]).astype(BF16) for c in each]
    grad_hidden = [dot(w2b[c], plain[c]) for c in each]
    slope = [
        half[c]
        + (0.5 * CURVE) * pre[c] * (1.0 - bend[c] * bend[c]) * (1.0 + (3.0 * CUBIC) * square[c])
        for c in each
    ]
    scaled_inner = [(grad_hidden[c] * slope[c] * rates[c]).astype(BF16) for c in each]
    ones = jnp.ones((TILE, TILE), BF16)
    for c in each:
        new = w1[c] - dot(scaled_inner[c], wide[c], NT)
        w1[c] = new
        w1b[c] = split_bias(new)
    for c in each:
        new = w2t[c] - dot(scaled_outer[c], hidden[c], NT)
        w2t[c] = new
        w2tb[c] = new.astype(BF16)
        bias2[c] = bias2[c] - dot(scaled_outer[c], ones, NT)
        new = w2[c] - dot(hidden[c], scaled_outer[c], NT)
        w2[c] = new
        w2b[c] = new.astype(BF16)
    return answer


def chain_kernel(tiles, count, x, first, second, second_t, bias, gain, shift, out,
                 w1, w2, w2t, w1b, w2b, w2tb, bias2, low):
    state = (w1, w2, w2t, w1b, w2b, w2tb)
    load_state(count, first, second, second_t, state)
    bias2[...] = bias[...]
    low[...] = jnp.zeros_like(low)
    consts = (gain, shift)
    lane = lax.broadcasted_iota(jnp.int32, (HEAD, TILE), 1)

    def finish(tile, answer):
        for c in range(count):
            out[tile, c] = jnp.where(lane < MB, low[c], answer[c]).astype(BF16)

    def body(tile, carry):
        before = jnp.maximum(tile - 1, 0)
        answer = mini_batch(
            count, True, True, x.at[tile], x.at[before], consts, state, bias2
        )
        finish(before, answer)
        answer = mini_batch(
            count, False, True, x.at[tile], x.at[tile], consts, state, bias2
        )
        for c in range(count):
            low[c] = answer[c]
        return carry

    lax.fori_loop(0, tiles, body, 0)
    answer = mini_batch(
        count, True, False, x.at[tiles - 1], x.at[tiles - 1], consts, state, bias2
    )
    finish(tiles - 1, answer)


def run_chains(x, first, second, second_t, bias, gain, shift):
    tiles, count = x.shape[:2]
    inner = second.shape[1]
    vmem = pl.BlockSpec(memory_space=pltpu.VMEM)
    return pl.pallas_call(
        functools.partial(chain_kernel, tiles, count),
        out_shape=jax.ShapeDtypeStruct((tiles, count, HEAD, TILE), BF16),
        in_specs=[vmem] * 7,
        out_specs=vmem,
        scratch_shapes=[
            pltpu.VMEM((count, inner, TILE), F32),
            pltpu.VMEM((count, inner, HEAD), F32),
            pltpu.VMEM((count, HEAD, inner), F32),
            pltpu.VMEM((count, inner, TILE), BF16),
            pltpu.VMEM((count, inner, HEAD), BF16),
            pltpu.VMEM((count, HEAD, inner), BF16),
            pltpu.VMEM((count, HEAD, TILE), F32),
            pltpu.VMEM((count, HEAD, TILE), F32),
        ],
        compiler_params=pltpu.CompilerParams(vmem_limit_bytes=32 * 1024 * 1024),
    )(x, first, second, second_t, bias, gain, shift)


def chain_params(heads, count, first_w, first_b, second_w, second_b, norm_gain, norm_shift, total):
    ids = jnp.minimum(lax.axis_index("seq") * count + jnp.arange(count), total - 1) % heads
    inner = first_w.shape[2]

    def pick(member):
        return jnp.take(member, ids, axis=0)

    def column(member):
        return jnp.broadcast_to(pick(member)[:, :, None], (count, HEAD, TILE))

    bias_lanes = jnp.broadcast_to(pick(first_b)[:, :, None], (count, inner, 2))
    first = jnp.concatenate(
        [
            jnp.swapaxes(pick(first_w), 1, 2),
            bias_lanes,
            jnp.zeros((count, inner, TILE - HEAD - 2), F32),
        ],
        axis=2,
    )
    second = pick(second_w)
    return (
        first, second, jnp.swapaxes(second, 1, 2),
        column(second_b), column(norm_gain), column(norm_shift),
    )


def shards(
    tokens,
    qkv_weight,
    rate_weight,
    base_rate,
    first_w,
    first_b,
    second_w,
    second_b,
    norm_gain,
    norm_shift,
    out_weight,
):
    places = lax.axis_size("seq")
    seqs, _, width = tokens.shape
    block = tokens.shape[1] * lax.axis_size("tensor")
    heads = first_w.shape[0]
    assert block % TILE == 0
    parts = block // TILE
    total = seqs * heads
    count = -(-total // places)
    params = chain_params(
        heads, count, first_w, first_b, second_w, second_b, norm_gain, norm_shift, total
    )
    piece = lax.all_gather(tokens, "tensor", axis=1, tiled=True)
    contract = (((1,), (2,)), ((), ()))
    projected = lax.dot_general(
        qkv_weight.reshape(-1, width), piece, contract, preferred_element_type=F32
    ).astype(BF16)
    projected = projected.reshape(heads, 3 * HEAD, seqs, block).transpose(2, 0, 1, 3)
    logit = lax.dot_general(rate_weight, piece, contract, preferred_element_type=F32)
    rates = (base_rate[:, None, None] * jax.nn.sigmoid(logit)).transpose(1, 0, 2)[:, :, None, :]
    coarse = lax.reduce_precision(rates, 8, 7)
    load = jnp.concatenate(
        [
            projected,
            coarse.astype(BF16),
            (rates - coarse).astype(BF16),
            jnp.zeros((seqs, heads, 14, block), BF16),
        ],
        axis=2,
    ).reshape(total, ROWS, block)
    load = jnp.pad(load, ((0, places * count - total), (0, 0), (0, 0)))
    load = load.reshape(places, count, ROWS, block)
    arrived = lax.all_to_all(load, "seq", 0, 0)
    arrived = arrived.reshape(places, count, ROWS, parts, TILE).transpose(0, 3, 1, 2, 4)
    answers = run_chains(arrived.reshape(places * parts, count, ROWS, TILE), *params)
    answers = answers.reshape(places, parts, count, HEAD, TILE).transpose(0, 2, 3, 1, 4)
    answers = lax.all_to_all(answers.reshape(places, count, HEAD, block), "seq", 0, 0)
    answers = answers.reshape(places * count, HEAD, block)[:total]
    answers = answers.reshape(seqs, heads * HEAD, block)
    partial = lax.dot_general(
        answers, out_weight, (((1,), (0,)), ((), ())), preferred_element_type=F32
    ).astype(BF16)
    return lax.psum_scatter(partial, "tensor", scatter_dimension=1, tiled=True)


def solution(mesh):
    in_specs = (
        P(None, ("seq", "tensor"), None),
        P("tensor", None, None),
        P("tensor", None),
        P("tensor"),
        P("tensor", None, None),
        P("tensor", None),
        P("tensor", None, None),
        P("tensor", None),
        P("tensor", None),
        P("tensor", None),
        P("tensor", None),
    )
    out_specs = P(None, ("seq", "tensor"), None)
    return jax.shard_map(shards, mesh=mesh, in_specs=in_specs, out_specs=out_specs, check_vma=False)
```

```python
import functools
import math

import jax
import jax.numpy as jnp
from jax import lax
from jax.experimental import pallas as pl
from jax.experimental.pallas import tpu as pltpu
from jax.sharding import PartitionSpec as P

HEAD = 64
MB = 64
TILE = 128
PAIRS = 8
CURVE = math.sqrt(2.0 / math.pi)
CUBIC = 0.044715
F32 = jnp.float32
BF16 = jnp.bfloat16
MESH = pl.DeviceIdType.MESH
NN = (((1,), (0,)), ((), ()))
NT = (((1,), (1,)), ((), ()))


def dot(a, b, dims=NN):
    return lax.dot_general(a, b, dims, preferred_element_type=F32)


def split_bias(state):
    lane = lax.broadcasted_iota(jnp.int32, state.shape, 1)
    rest = state - state.astype(BF16).astype(F32)
    return jnp.where(lane == HEAD + 1, rest, state).astype(BF16)


def mean_rows(values):
    return jnp.sum(values, axis=0, keepdims=True) * (1.0 / HEAD)


def load_state(count, first, second, second_t, state):
    w1, w2, w2t, w1b, w2b, w2tb = state
    for c in range(count):
        w1[c] = first[c]
        w2[c] = second[c]
        w2t[c] = second_t[c]
        w1b[c] = split_bias(first[c])
        w2b[c] = second[c].astype(BF16)
        w2tb[c] = second_t[c].astype(BF16)


def rows_of(tile, chain, kind):
    start = (3 * chain + kind) * HEAD
    return tile[start : start + HEAD, :]


def mini_batch(count, keys_low, learn, key_tile, query_tile, consts, state, bias2):
    gain, shift = consts
    w1, w2, w2t, w1b, w2b, w2tb = state
    each = range(count)
    lane = lax.broadcasted_iota(jnp.int32, (HEAD, TILE), 1)
    is_key = (lane < MB) if keys_low else (lane >= MB)
    row = lax.broadcasted_iota(jnp.int32, (HEAD, TILE), 0)
    ones_rows = jnp.where(row < 2, 1.0, 0.0)
    rows = [
        jnp.where(
            is_key,
            rows_of(key_tile, c, 1).astype(F32),
            rows_of(query_tile, c, 0).astype(F32),
        )
        for c in each
    ]
    wide = [jnp.concatenate([rows[c], ones_rows], axis=0).astype(BF16) for c in each]
    pre = [dot(w1b[c], wide[c]) for c in each]
    square = [p * p for p in pre]
    bend = [jnp.tanh((CURVE * p) * (1.0 + CUBIC * s)) for p, s in zip(pre, square)]
    half = [0.5 + 0.5 * t for t in bend]
    hidden = [(p * h).astype(BF16) for p, h in zip(pre, half)]
    outer = [dot(w2tb[c], hidden[c]) + bias2[c] for c in each]
    centered = [o - mean_rows(o) for o in outer]
    inverse = [lax.rsqrt(mean_rows(z * z) + 1e-06) for z in centered]
    normed = [z * i for z, i in zip(centered, inverse)]
    model = [gain[c] * normed[c] + shift[c] for c in each]
    answer = [rows[c] + model[c] for c in each]
    if not learn:
        return answer
    values = [rows_of(key_tile, c, 2).astype(F32) for c in each]
    upstream = [(model[c] - (values[c] - rows[c])) * gain[c] for c in each]
    grad_outer = [
        inverse[c]
        * (
            upstream[c]
            - mean_rows(upstream[c])
            - normed[c] * mean_rows(upstream[c] * normed[c])
        )
        for c in each
    ]
    rates = []
    tail = 3 * HEAD * count
    pairs = key_tile[tail : tail + 2 * PAIRS, :].astype(F32)
    for c in each:
        rate = pairs[c : c + 1, :] + pairs[PAIRS + c : PAIRS + c + 1, :]
        rates.append(jnp.where(is_key[0:1, :], rate, 0.0))
    plain = [g.astype(BF16) for g in grad_outer]
    scaled_outer = [(rates[c] * grad_outer[c]).astype(BF16) for c in each]
    grad_hidden = [dot(w2b[c], plain[c]) for c in each]
    slope = [
        half[c]
        + (0.5 * CURVE) * pre[c] * (1.0 - bend[c] * bend[c]) * (1.0 + (3.0 * CUBIC) * square[c])
        for c in each
    ]
    scaled_inner = [(grad_hidden[c] * slope[c] * rates[c]).astype(BF16) for c in each]
    ones = jnp.ones((TILE, TILE), BF16)
    for c in each:
        new = w1[c] - dot(scaled_inner[c], wide[c], NT)
        w1[c] = new
        w1b[c] = split_bias(new)
    for c in each:
        new = w2t[c] - dot(scaled_outer[c], hidden[c], NT)
        w2t[c] = new
        w2tb[c] = new.astype(BF16)
        bias2[c] = bias2[c] - dot(scaled_outer[c], ones, NT)
        new = w2[c] - dot(hidden[c], scaled_outer[c], NT)
        w2[c] = new
        w2b[c] = new.astype(BF16)
    return answer


def flipped(index, bits, count):
    result = 0
    place = 1
    while place < count:
        bit = lax.rem(index // place, 2)
        result = result + place * ((1 - bit) if (bits // place) % 2 else bit)
        place *= 2
    return result


def partner(index, step, count):
    if count & (count - 1) == 0:
        return flipped(index, step, count)
    return lax.rem(index + step, count)


def greet(axis, count):
    me = lax.axis_index(axis)
    barrier = pltpu.get_barrier_semaphore()
    for step in range(1, count):
        pl.semaphore_signal(
            barrier, inc=1, device_id={axis: partner_all(me, step, count)}, device_id_type=MESH
        )
    pl.semaphore_wait(barrier, count - 1)
    return me


def partner_all(index, step, count):
    return lax.rem(index + step, count)


def gather_kernel(group, seqs, mine, out, send_sem, recv_sem, own_sem):
    me = greet("tensor", group)
    copies = []
    for step in range(group - 1, 0, -1):
        peer = partner(me, step, group)
        for s in range(seqs):
            copy = pltpu.make_async_remote_copy(
                src_ref=mine.at[s],
                dst_ref=out.at[s, me],
                send_sem=send_sem.at[step, s],
                recv_sem=recv_sem.at[s, me],
                device_id={"tensor": peer},
                device_id_type=MESH,
            )
            copy.start()
            copies.append(copy)
    own = [pltpu.make_async_copy(mine.at[s], out.at[s, me], own_sem.at[s]) for s in range(seqs)]
    for copy in own:
        copy.start()
    for copy in own:
        copy.wait()
    for step in range(group - 1, 0, -1):
        peer = partner(me, step, group)
        for s in range(seqs):
            pltpu.make_async_remote_copy(
                src_ref=mine.at[s],
                dst_ref=out.at[s, peer],
                send_sem=send_sem.at[step, s],
                recv_sem=recv_sem.at[s, peer],
                device_id={"tensor": peer},
                device_id_type=MESH,
            ).wait_recv()
    for copy in copies:
        copy.wait_send()


def gather_tokens(tokens):
    group = lax.axis_size("tensor")
    seqs, own, width = tokens.shape
    spec = pl.BlockSpec(memory_space=pl.ANY)
    out = pl.pallas_call(
        functools.partial(gather_kernel, group, seqs),
        out_shape=jax.ShapeDtypeStruct((seqs, group, own, width), BF16),
        in_specs=[spec],
        out_specs=spec,
        scratch_shapes=[
            pltpu.SemaphoreType.DMA((group, seqs)),
            pltpu.SemaphoreType.DMA((seqs, group)),
            pltpu.SemaphoreType.DMA((seqs,)),
        ],
        compiler_params=pltpu.CompilerParams(collective_id=1, has_side_effects=True),
    )(tokens)
    return out.reshape(seqs, group * own, width)


def chain_kernel(places, parts, count, x, first, second, second_t, bias, gain, shift, back,
                 w1, w2, w2t, w1b, w2b, w2tb, bias2, low, arrive, outs,
                 send_sem, recv_sem, own_sem, back_send, back_recv, back_own):
    me = greet("seq", places)

    def forward(step, peer, source):
        return pltpu.make_async_remote_copy(
            src_ref=x.at[peer],
            dst_ref=arrive.at[source],
            send_sem=send_sem.at[step],
            recv_sem=recv_sem.at[source],
            device_id={"seq": peer},
            device_id_type=MESH,
        )

    def homeward(place, source):
        return pltpu.make_async_remote_copy(
            src_ref=outs.at[place],
            dst_ref=back.at[source],
            send_sem=back_send.at[place],
            recv_sem=back_recv.at[source],
            device_id={"seq": place},
            device_id_type=MESH,
        )

    for step in range(places - 1, 0, -1):
        forward(step, partner(me, step, places), me).start()
    own = pltpu.make_async_copy(x.at[me], arrive.at[me], own_sem)
    own.start()
    own_back = pltpu.make_async_copy(outs.at[me], back.at[me], back_own)
    state = (w1, w2, w2t, w1b, w2b, w2tb)
    load_state(count, first, second, second_t, state)
    bias2[...] = bias[...]
    low[...] = jnp.zeros_like(low)
    consts = (gain, shift)
    lane = lax.broadcasted_iota(jnp.int32, (HEAD, TILE), 1)

    def finish(place, part, answer):
        for c in range(count):
            outs[place, part, c * HEAD : (c + 1) * HEAD, :] = jnp.where(
                lane < MB, low[c], answer[c]
            ).astype(BF16)

    def send_home(place):
        @pl.when(place == me)
        def _():
            own_back.start()

        @pl.when(place != me)
        def _():
            homeward(place, me).start()

    def body(place, carry):
        @pl.when(place == me)
        def _():
            own.wait()

        @pl.when(place != me)
        def _():
            forward(0, place, place).wait_recv()

        for part in range(parts):
            tile = arrive.at[place, part]
            if part:
                old_place, old_part = place, part - 1
            else:
                old_place, old_part = jnp.maximum(place - 1, 0), parts - 1
            before = arrive.at[old_place, old_part]
            answer = mini_batch(count, True, True, tile, before, consts, state, bias2)
            finish(old_place, old_part, answer)
            if not part:

                @pl.when(place > 0)
                def _():
                    send_home(place - 1)

            answer = mini_batch(count, False, True, tile, tile, consts, state, bias2)
            for c in range(count):
                low[c] = answer[c]
        return carry

    lax.fori_loop(0, places, body, 0)
    last = arrive.at[places - 1, parts - 1]
    answer = mini_batch(count, True, False, last, last, consts, state, bias2)
    finish(places - 1, parts - 1, answer)
    send_home(places - 1)
    own_back.wait()
    for step in range(1, places):
        peer = partner(me, step, places)
        forward(step, peer, me).wait_send()
        homeward(peer, peer).wait_recv()
        homeward(peer, me).wait_send()


def run_chains(x, count, first, second, second_t, bias, gain, shift):
    places, parts, rows = x.shape[:3]
    inner = second.shape[1]
    vmem = pl.BlockSpec(memory_space=pltpu.VMEM)
    whole = pl.BlockSpec(memory_space=pl.ANY)
    return pl.pallas_call(
        functools.partial(chain_kernel, places, parts, count),
        out_shape=jax.ShapeDtypeStruct((places, parts, count * HEAD, TILE), BF16),
        in_specs=[whole] + [vmem] * 6,
        out_specs=whole,
        scratch_shapes=[
            pltpu.VMEM((count, inner, TILE), F32),
            pltpu.VMEM((count, inner, HEAD), F32),
            pltpu.VMEM((count, HEAD, inner), F32),
            pltpu.VMEM((count, inner, TILE), BF16),
            pltpu.VMEM((count, inner, HEAD), BF16),
            pltpu.VMEM((count, HEAD, inner), BF16),
            pltpu.VMEM((count, HEAD, TILE), F32),
            pltpu.VMEM((count, HEAD, TILE), F32),
            pltpu.VMEM((places, parts, rows, TILE), BF16),
            pltpu.VMEM((places, parts, count * HEAD, TILE), BF16),
            pltpu.SemaphoreType.DMA((places,)),
            pltpu.SemaphoreType.DMA((places,)),
            pltpu.SemaphoreType.DMA,
            pltpu.SemaphoreType.DMA((places,)),
            pltpu.SemaphoreType.DMA((places,)),
            pltpu.SemaphoreType.DMA,
        ],
        compiler_params=pltpu.CompilerParams(
            collective_id=2, has_side_effects=True, vmem_limit_bytes=32 * 1024 * 1024
        ),
    )(x, first, second, second_t, bias, gain, shift)


def mix_kernel(group, cuts, rows_ref, weight, out, ready, land, send_sem, recv_sem):
    me = greet("tensor", group)
    own, width = out.shape
    piece = width // cuts

    def move(cut, step, peer):
        return pltpu.make_async_remote_copy(
            src_ref=ready.at[cut, peer],
            dst_ref=land.at[cut, step],
            send_sem=send_sem.at[cut, step],
            recv_sem=recv_sem.at[cut, step],
            device_id={"tensor": peer},
            device_id_type=MESH,
        )

    for cut in range(cuts):
        part = dot(rows_ref[...], weight[:, cut * piece : (cut + 1) * piece])
        ready[cut] = part.astype(BF16).reshape(group, own, piece)
        for step in range(group - 1, 0, -1):
            move(cut, step, partner(me, step, group)).start()
    for cut in range(cuts):
        total = ready[cut, me].astype(F32)
        for step in range(group - 1, 0, -1):
            move(cut, step, partner(me, step, group)).wait_recv()
            total = total + land[cut, step].astype(F32)
        out[:, cut * piece : (cut + 1) * piece] = total.astype(BF16)
    for cut in range(cuts):
        for step in range(group - 1, 0, -1):
            move(cut, step, partner(me, step, group)).wait_send()


def mix_heads(rows, weight):
    group = lax.axis_size("tensor")
    own = rows.shape[0] // group
    width = weight.shape[1]
    cuts = 6
    piece = width // cuts
    vmem = pl.BlockSpec(memory_space=pltpu.VMEM)
    return pl.pallas_call(
        functools.partial(mix_kernel, group, cuts),
        out_shape=jax.ShapeDtypeStruct((own, width), BF16),
        in_specs=[vmem, vmem],
        out_specs=vmem,
        scratch_shapes=[
            pltpu.VMEM((cuts, group, own, piece), BF16),
            pltpu.VMEM((cuts, group, own, piece), BF16),
            pltpu.SemaphoreType.DMA((cuts, group)),
            pltpu.SemaphoreType.DMA((cuts, group)),
        ],
        compiler_params=pltpu.CompilerParams(
            collective_id=3, has_side_effects=True, vmem_limit_bytes=32 * 1024 * 1024
        ),
    )(rows, weight)


def chain_params(heads, count, first_w, first_b, second_w, second_b, norm_gain, norm_shift, total):
    ids = jnp.minimum(lax.axis_index("seq") * count + jnp.arange(count), total - 1) % heads
    inner = first_w.shape[2]

    def pick(member):
        return jnp.take(member, ids, axis=0)

    def column(member):
        return jnp.broadcast_to(pick(member)[:, :, None], (count, HEAD, TILE))

    bias_lanes = jnp.broadcast_to(pick(first_b)[:, :, None], (count, inner, 2))
    first = jnp.concatenate(
        [
            jnp.swapaxes(pick(first_w), 1, 2),
            bias_lanes,
            jnp.zeros((count, inner, TILE - HEAD - 2), F32),
        ],
        axis=2,
    )
    second = pick(second_w)
    return (
        first, second, jnp.swapaxes(second, 1, 2),
        column(second_b), column(norm_gain), column(norm_shift),
    )


def shards(
    tokens,
    qkv_weight,
    rate_weight,
    base_rate,
    first_w,
    first_b,
    second_w,
    second_b,
    norm_gain,
    norm_shift,
    out_weight,
):
    places = lax.axis_size("seq")
    seqs, _, width = tokens.shape
    block = tokens.shape[1] * lax.axis_size("tensor")
    heads = first_w.shape[0]
    assert block % TILE == 0
    parts = block // TILE
    total = seqs * heads
    count = -(-total // places)
    assert count <= PAIRS
    params = chain_params(
        heads, count, first_w, first_b, second_w, second_b, norm_gain, norm_shift, total
    )
    piece = gather_tokens(tokens)
    contract = (((1,), (2,)), ((), ()))
    projected = lax.dot_general(
        qkv_weight.reshape(-1, width), piece, contract, preferred_element_type=F32
    ).astype(BF16)
    projected = projected.reshape(heads, 3 * HEAD, seqs, block).transpose(2, 0, 1, 3)
    logit = lax.dot_general(rate_weight, piece, contract, preferred_element_type=F32)
    rates = (base_rate[:, None, None] * jax.nn.sigmoid(logit)).transpose(1, 0, 2)

    def by_place(member):
        member = member.reshape((total,) + member.shape[2:])
        extra = places * count - total
        if extra:
            member = jnp.pad(member, ((0, extra),) + ((0, 0),) * (member.ndim - 1))
        return member.reshape((places, -1, block))

    coarse = lax.reduce_precision(rates, 8, 7)
    fill = jnp.zeros((places, PAIRS - count, block), BF16)
    load = jnp.concatenate(
        [
            by_place(projected),
            by_place(coarse.astype(BF16)),
            fill,
            by_place((rates - coarse).astype(BF16)),
            fill,
        ],
        axis=1,
    )
    load = load.reshape(places, -1, parts, TILE).transpose(0, 2, 1, 3)
    answers = run_chains(load, count, *params)
    answers = answers.transpose(0, 2, 1, 3).reshape(places * count, HEAD, block)[:total]
    group = lax.axis_size("tensor")
    rows = answers.reshape(seqs, heads * HEAD, group, block // group)
    rows = rows.transpose(2, 0, 3, 1).reshape(-1, heads * HEAD)
    return mix_heads(rows, out_weight).reshape(tokens.shape)


def solution(mesh):
    in_specs = (
        P(None, ("seq", "tensor"), None),
        P("tensor", None, None),
        P("tensor", None),
        P("tensor"),
        P("tensor", None, None),
        P("tensor", None),
        P("tensor", None, None),
        P("tensor", None),
        P("tensor", None),
        P("tensor", None),
        P("tensor", None),
    )
    out_specs = P(None, ("seq", "tensor"), None)
    return jax.shard_map(shards, mesh=mesh, in_specs=in_specs, out_specs=out_specs, check_vma=False)
```

```python
import functools
import math

import jax
import jax.numpy as jnp
from jax import lax
from jax.experimental import pallas as pl
from jax.experimental.pallas import tpu as pltpu
from jax.sharding import PartitionSpec as P

HEAD = 64
MB = 64
TILE = 128
PAIRS = 8
CURVE = math.sqrt(2.0 / math.pi)
CUBIC = 0.044715
F32 = jnp.float32
BF16 = jnp.bfloat16
MESH = pl.DeviceIdType.MESH
NN = (((1,), (0,)), ((), ()))
NT = (((1,), (1,)), ((), ()))


def dot(a, b, dims=NN):
    return lax.dot_general(a, b, dims, preferred_element_type=F32)


def split_bias(state):
    lane = lax.broadcasted_iota(jnp.int32, state.shape, 1)
    rest = state - state.astype(BF16).astype(F32)
    return jnp.where(lane == HEAD + 1, rest, state).astype(BF16)


def mean_rows(values):
    return jnp.sum(values, axis=0, keepdims=True) * (1.0 / HEAD)


def load_state(me, count, total, params, consts, state, bias2):
    first_w, first_b, second_w, second_b, norm_gain, norm_shift = params
    gain, shift = consts
    w1, w2, w2t, w1b, w2b, w2tb = state
    inner = first_w.shape[2]

    def column(member, head):
        return jnp.broadcast_to(member[head], (TILE, HEAD)).T

    for c in range(count):
        head = lax.rem(jnp.minimum(me * count + c, total - 1), first_w.shape[0])
        row = first_b[head]
        fill = jnp.zeros((TILE - HEAD - 2, inner), F32)
        first = jnp.concatenate([first_w[head], row, row, fill], axis=0).T
        second = second_w[head]
        w1[c] = first
        w1b[c] = split_bias(first)
        w2[c] = second
        w2b[c] = second.astype(BF16)
        w2t[c] = second.T
        w2tb[c] = second.T.astype(BF16)
        bias2[c] = column(second_b, head)
        gain[c] = column(norm_gain, head)
        shift[c] = column(norm_shift, head)


def rows_of(tile, chain, kind):
    start = (3 * chain + kind) * HEAD
    return tile[start : start + HEAD, :]


def mini_batch(count, keys_low, learn, key_tile, query_tile, consts, state, bias2):
    gain, shift = consts
    w1, w2, w2t, w1b, w2b, w2tb = state
    each = range(count)
    lane = lax.broadcasted_iota(jnp.int32, (HEAD, TILE), 1)
    is_key = (lane < MB) if keys_low else (lane >= MB)
    row = lax.broadcasted_iota(jnp.int32, (HEAD, TILE), 0)
    ones_rows = jnp.where(row < 2, 1.0, 0.0)
    rows = [
        jnp.where(
            is_key,
            rows_of(key_tile, c, 1).astype(F32),
            rows_of(query_tile, c, 0).astype(F32),
        )
        for c in each
    ]
    wide = [jnp.concatenate([rows[c], ones_rows], axis=0).astype(BF16) for c in each]
    pre = [dot(w1b[c], wide[c]) for c in each]
    square = [p * p for p in pre]
    bend = [jnp.tanh((CURVE * p) * (1.0 + CUBIC * s)) for p, s in zip(pre, square)]
    half = [0.5 + 0.5 * t for t in bend]
    hidden = [(p * h).astype(BF16) for p, h in zip(pre, half)]
    outer = [dot(w2tb[c], hidden[c]) + bias2[c] for c in each]
    centered = [o - mean_rows(o) for o in outer]
    inverse = [lax.rsqrt(mean_rows(z * z) + 1e-06) for z in centered]
    normed = [z * i for z, i in zip(centered, inverse)]
    model = [gain[c] * normed[c] + shift[c] for c in each]
    answer = [rows[c] + model[c] for c in each]
    if not learn:
        return answer
    values = [rows_of(key_tile, c, 2).astype(F32) for c in each]
    upstream = [(model[c] - (values[c] - rows[c])) * gain[c] for c in each]
    grad_outer = [
        inverse[c]
        * (
            upstream[c]
            - mean_rows(upstream[c])
            - normed[c] * mean_rows(upstream[c] * normed[c])
        )
        for c in each
    ]
    rates = []
    tail = 3 * HEAD * count
    pairs = key_tile[tail : tail + 2 * PAIRS, :].astype(F32)
    for c in each:
        rate = pairs[c : c + 1, :] + pairs[PAIRS + c : PAIRS + c + 1, :]
        rates.append(jnp.where(is_key[0:1, :], rate, 0.0))
    plain = [g.astype(BF16) for g in grad_outer]
    scaled_outer = [(rates[c] * grad_outer[c]).astype(BF16) for c in each]
    grad_hidden = [dot(w2b[c], plain[c]) for c in each]
    slope = [
        half[c]
        + (0.5 * CURVE) * pre[c] * (1.0 - bend[c] * bend[c]) * (1.0 + (3.0 * CUBIC) * square[c])
        for c in each
    ]
    scaled_inner = [(grad_hidden[c] * slope[c] * rates[c]).astype(BF16) for c in each]
    ones = jnp.ones((TILE, TILE), BF16)
    for c in each:
        new = w1[c] - dot(scaled_inner[c], wide[c], NT)
        w1[c] = new
        w1b[c] = split_bias(new)
    for c in each:
        new = w2t[c] - dot(scaled_outer[c], hidden[c], NT)
        w2t[c] = new
        w2tb[c] = new.astype(BF16)
        bias2[c] = bias2[c] - dot(scaled_outer[c], ones, NT)
        new = w2[c] - dot(hidden[c], scaled_outer[c], NT)
        w2[c] = new
        w2b[c] = new.astype(BF16)
    return answer


def flipped(index, bits, count):
    result = 0
    place = 1
    while place < count:
        bit = lax.rem(index // place, 2)
        result = result + place * ((1 - bit) if (bits // place) % 2 else bit)
        place *= 2
    return result


def partner(index, step, count):
    if count & (count - 1) == 0:
        return flipped(index, step, count)
    return lax.rem(index + step, count)


def greet(axes):
    barrier = pltpu.get_barrier_semaphore()
    for axis, count in axes:
        me = lax.axis_index(axis)
        for step in range(1, count):
            pl.semaphore_signal(
                barrier,
                inc=1,
                device_id={axis: lax.rem(me + step, count)},
                device_id_type=MESH,
            )
    pl.semaphore_wait(barrier, sum(count - 1 for _, count in axes))


def block_of(heads):
    return max(n for n in (4, 3, 2, 1) if heads % n == 0)


def project(sizes, group_me, mine, qkv, rate_weight, base, load, weights, sums, land,
            weight_sem, token_send, token_recv):
    places, group, seqs, heads, parts, count, own, pieces = sizes
    piece = mine.shape[1] // pieces
    total = seqs * heads
    block = group * own
    several = block_of(heads)

    def span(cut):
        return slice(cut * piece, (cut + 1) * piece)

    def fetch(cut):
        return pltpu.make_async_copy(
            qkv.at[:, span(cut)], weights.at[cut], weight_sem.at[cut]
        )

    def move(cut, step, peer, source):
        return pltpu.make_async_remote_copy(
            src_ref=mine.at[:, span(cut)],
            dst_ref=land.at[cut, source],
            send_sem=token_send.at[cut, step],
            recv_sem=token_recv.at[cut, source],
            device_id={"tensor": peer},
            device_id_type=MESH,
        )

    for cut in range(pieces):
        for step in range(group - 1, 0, -1):
            move(cut, step, partner(group_me, step, group), group_me).start()
    for cut in range(pieces):
        fetch(cut).start()
    yield
    logit = None
    for cut in range(pieces):
        land[cut, group_me] = mine[:, span(cut)]
        fetch(cut).wait()
        for step in range(group - 1, 0, -1):
            peer = partner(group_me, step, group)
            move(cut, step, peer, peer).wait_recv()
        wide = land[cut].astype(F32)
        tokens = jnp.concatenate(
            [wide[:, n * own : (n + 1) * own].reshape(block, piece) for n in range(seqs)], axis=0
        ).astype(BF16)
        more = dot(rate_weight[:, span(cut)], tokens, NT)
        logit = more if logit is None else logit + more

        def some_heads(index, carry):
            rows = pl.ds(pl.multiple_of(index * (several * 3 * HEAD), 64), several * 3 * HEAD)
            part = dot(weights[cut, rows, :], tokens, NT)
            part = part.reshape(several, 3 * HEAD, seqs * block)
            at = pl.ds(index * several, several)
            sums[at] = part if cut == 0 else sums[at] + part
            return carry

        lax.fori_loop(0, heads // several, some_heads, 0)
    if places * count > total:
        load[...] = jnp.zeros_like(load)
    rates = base[...][:, :1] * jax.nn.sigmoid(logit)
    for place in range(places):
        for part in range(parts):
            coarse, fine = [], []
            for c in range(count):
                chain = place * count + c
                if chain >= total:
                    break
                n, head = chain // heads, chain % heads
                lanes = slice(n * block + part * TILE, n * block + (part + 1) * TILE)
                load[place, part, c * 3 * HEAD : (c + 1) * 3 * HEAD, :] = sums[
                    head, :, lanes
                ].astype(BF16)
                row = rates[head : head + 1, lanes]
                short = row.astype(BF16).astype(F32)
                coarse.append(short)
                fine.append(row - short)
            if coarse:
                fill = [jnp.zeros((PAIRS - len(coarse), TILE), F32)]
                load[place, part, count * 3 * HEAD :, :] = jnp.concatenate(
                    coarse + fill + fine + fill, axis=0
                ).astype(BF16)
    for cut in range(pieces):
        for step in range(group - 1, 0, -1):
            move(cut, step, partner(group_me, step, group), group_me).wait_send()


def layer_kernel(sizes, mine, qkv, rate_weight, base, first_w, first_b, second_w, second_b,
                 norm_gain, norm_shift, mix_weight, out,
                 w1, w2, w2t, w1b, w2b, w2tb, bias2, low, gain, shift,
                 x, arrive, outs, back, weights, sums, land, mix, ready, shares,
                 weight_sem, token_send, token_recv, mix_sem,
                 send_sem, recv_sem, own_sem, back_send, back_recv, back_own,
                 share_send, share_recv):
    places, group, seqs, heads, parts, count, own_rows, pieces = sizes
    total_chains = seqs * heads
    me = lax.axis_index("seq")
    group_me = lax.axis_index("tensor")
    greet((("tensor", group), ("seq", places)))
    front = project(
        sizes, group_me, mine, qkv, rate_weight, base, x, weights, sums, land,
        weight_sem, token_send, token_recv,
    )
    next(front)
    mix_copy = pltpu.make_async_copy(mix_weight, mix, mix_sem)
    mix_copy.start()
    state = (w1, w2, w2t, w1b, w2b, w2tb)
    consts = (gain, shift)
    params = (first_w, first_b, second_w, second_b, norm_gain, norm_shift)
    load_state(me, count, total_chains, params, consts, state, bias2)
    low[...] = jnp.zeros_like(low)
    for _ in front:
        pass

    def forward(step, peer, source):
        return pltpu.make_async_remote_copy(
            src_ref=x.at[peer],
            dst_ref=arrive.at[source],
            send_sem=send_sem.at[step],
            recv_sem=recv_sem.at[source],
            device_id={"seq": peer},
            device_id_type=MESH,
        )

    def homeward(place, source):
        return pltpu.make_async_remote_copy(
            src_ref=outs.at[place],
            dst_ref=back.at[source],
            send_sem=back_send.at[place],
            recv_sem=back_recv.at[source],
            device_id={"seq": place},
            device_id_type=MESH,
        )

    for step in range(places - 1, 0, -1):
        forward(step, partner(me, step, places), me).start()
    own = pltpu.make_async_copy(x.at[me], arrive.at[me], own_sem)
    own.start()
    own_back = pltpu.make_async_copy(outs.at[me], back.at[me], back_own)
    lane = lax.broadcasted_iota(jnp.int32, (HEAD, TILE), 1)

    def finish(place, part, answer):
        for c in range(count):
            outs[place, part, c * HEAD : (c + 1) * HEAD, :] = jnp.where(
                lane < MB, low[c], answer[c]
            ).astype(BF16)

    def send_home(place):
        @pl.when(place == me)
        def _():
            own_back.start()

        @pl.when(place != me)
        def _():
            homeward(place, me).start()

    def body(place, carry):
        @pl.when(place == me)
        def _():
            own.wait()

        @pl.when(place != me)
        def _():
            forward(0, place, place).wait_recv()

        for part in range(parts):
            tile = arrive.at[place, part]
            if part:
                old_place, old_part = place, part - 1
            else:
                old_place, old_part = jnp.maximum(place - 1, 0), parts - 1
            before = arrive.at[old_place, old_part]
            answer = mini_batch(count, True, True, tile, before, consts, state, bias2)
            finish(old_place, old_part, answer)
            if not part:

                @pl.when(place > 0)
                def _():
                    send_home(place - 1)

            answer = mini_batch(count, False, True, tile, tile, consts, state, bias2)
            for c in range(count):
                low[c] = answer[c]
        return carry

    lax.fori_loop(0, places, body, 0)
    last = arrive.at[places - 1, parts - 1]
    answer = mini_batch(count, True, False, last, last, consts, state, bias2)
    finish(places - 1, parts - 1, answer)
    send_home(places - 1)
    own_back.wait()
    for step in range(1, places):
        peer = partner(me, step, places)
        forward(step, peer, me).wait_send()
        homeward(peer, peer).wait_recv()
        homeward(peer, me).wait_send()


    mix_copy.wait()
    flat = back[...]
    flat = jnp.concatenate(
        [flat[:, part].reshape(places * count * HEAD, TILE) for part in range(parts)], axis=1
    )
    feats = heads * HEAD
    rows = [flat[n * feats : (n + 1) * feats].astype(F32).T.astype(BF16) for n in range(seqs)]
    width = mix.shape[1]
    cuts = ready.shape[0]
    piece = width // cuts

    def move(cut, step, peer):
        return pltpu.make_async_remote_copy(
            src_ref=ready.at[cut, peer],
            dst_ref=shares.at[cut, step],
            send_sem=share_send.at[cut, step],
            recv_sem=share_recv.at[cut, step],
            device_id={"tensor": peer},
            device_id_type=MESH,
        )

    both = jnp.concatenate(rows, axis=0)
    for cut in range(cuts):
        part = dot(both, mix[:, cut * piece : (cut + 1) * piece])
        part = part.reshape(seqs, group, own_rows, piece)
        ready[cut] = jnp.concatenate([part[n] for n in range(seqs)], axis=1).astype(BF16)
        for step in range(group - 1, 0, -1):
            move(cut, step, partner(group_me, step, group)).start()
    for cut in range(cuts):
        result = ready[cut, group_me].astype(F32)
        for step in range(group - 1, 0, -1):
            move(cut, step, partner(group_me, step, group)).wait_recv()
            result = result + shares[cut, step].astype(F32)
        out[:, cut * piece : (cut + 1) * piece] = result.astype(BF16)
    for cut in range(cuts):
        for step in range(group - 1, 0, -1):
            move(cut, step, partner(group_me, step, group)).wait_send()


def shards(
    tokens,
    qkv_weight,
    rate_weight,
    base_rate,
    first_w,
    first_b,
    second_w,
    second_b,
    norm_gain,
    norm_shift,
    out_weight,
):
    places = lax.axis_size("seq")
    group = lax.axis_size("tensor")
    seqs, own, width = tokens.shape
    block = own * group
    heads, _, inner = first_w.shape
    assert block % TILE == 0
    parts = block // TILE
    count = -(-seqs * heads // places)
    assert count <= PAIRS
    pieces = cuts = 6
    piece = width // pieces
    sizes = (places, group, seqs, heads, parts, count, own, pieces)
    vmem = pl.BlockSpec(memory_space=pltpu.VMEM)
    whole = pl.BlockSpec(memory_space=pl.ANY)
    dma = pltpu.SemaphoreType.DMA
    rows = count * 3 * HEAD + 2 * PAIRS
    out = pl.pallas_call(
        functools.partial(layer_kernel, sizes),
        out_shape=jax.ShapeDtypeStruct((seqs * own, width), BF16),
        in_specs=[vmem, whole] + [vmem] * 8 + [whole],
        out_specs=vmem,
        scratch_shapes=[
            pltpu.VMEM((count, inner, TILE), F32),
            pltpu.VMEM((count, inner, HEAD), F32),
            pltpu.VMEM((count, HEAD, inner), F32),
            pltpu.VMEM((count, inner, TILE), BF16),
            pltpu.VMEM((count, inner, HEAD), BF16),
            pltpu.VMEM((count, HEAD, inner), BF16),
            pltpu.VMEM((count, HEAD, TILE), F32),
            pltpu.VMEM((count, HEAD, TILE), F32),
            pltpu.VMEM((count, HEAD, TILE), F32),
            pltpu.VMEM((count, HEAD, TILE), F32),
            pltpu.VMEM((places, parts, rows, TILE), BF16),
            pltpu.VMEM((places, parts, rows, TILE), BF16),
            pltpu.VMEM((places, parts, count * HEAD, TILE), BF16),
            pltpu.VMEM((places, parts, count * HEAD, TILE), BF16),
            pltpu.VMEM((pieces, heads * 3 * HEAD, piece), BF16),
            pltpu.VMEM((heads, 3 * HEAD, seqs * block), F32),
            pltpu.VMEM((pieces, group, seqs * own, piece), BF16),
            pltpu.VMEM((heads * HEAD, width), BF16),
            pltpu.VMEM((cuts, group, seqs * own, width // cuts), BF16),
            pltpu.VMEM((cuts, group, seqs * own, width // cuts), BF16),
            dma((pieces,)),
            dma((pieces, group)),
            dma((pieces, group)),
            dma,
            dma((places,)),
            dma((places,)),
            dma,
            dma((places,)),
            dma((places,)),
            dma,
            dma((cuts, group)),
            dma((cuts, group)),
        ],
        compiler_params=pltpu.CompilerParams(
            collective_id=1, has_side_effects=True, vmem_limit_bytes=56 * 1024 * 1024
        ),
    )(
        tokens.reshape(seqs * own, width),
        qkv_weight.reshape(-1, width),
        rate_weight,
        jnp.broadcast_to(base_rate[:, None], (heads, TILE)),
        first_w,
        first_b[:, None],
        second_w,
        second_b[:, None],
        norm_gain[:, None],
        norm_shift[:, None],
        out_weight,
    )
    return out.reshape(tokens.shape)


def solution(mesh):
    in_specs = (
        P(None, ("seq", "tensor"), None),
        P("tensor", None, None),
        P("tensor", None),
        P("tensor"),
        P("tensor", None, None),
        P("tensor", None),
        P("tensor", None, None),
        P("tensor", None),
        P("tensor", None),
        P("tensor", None),
        P("tensor", None),
    )
    out_specs = P(None, ("seq", "tensor"), None)
    return jax.shard_map(shards, mesh=mesh, in_specs=in_specs, out_specs=out_specs, check_vma=False)
```

```python
import functools
import math

import jax
import jax.numpy as jnp
from jax import lax
from jax.experimental import pallas as pl
from jax.experimental.pallas import tpu as pltpu
from jax.sharding import PartitionSpec as P

HEAD = 64
MB = 64
TILE = 128
PAIRS = 8
CURVE = math.sqrt(2.0 / math.pi)
CUBIC = 0.044715
F32 = jnp.float32
BF16 = jnp.bfloat16
MESH = pl.DeviceIdType.MESH
NN = (((1,), (0,)), ((), ()))
NT = (((1,), (1,)), ((), ()))


def dot(a, b, dims=NN):
    return lax.dot_general(a, b, dims, preferred_element_type=F32)


def split_bias(state):
    lane = lax.broadcasted_iota(jnp.int32, state.shape, 1)
    rest = state - state.astype(BF16).astype(F32)
    return jnp.where(lane == HEAD + 1, rest, state).astype(BF16)


def mean_rows(values):
    return jnp.sum(values, axis=0, keepdims=True) * (1.0 / HEAD)


def load_state(me, count, total, params, consts, state, bias2):
    first_w, first_b, second_w, second_b, norm_gain, norm_shift = params
    gain, shift = consts
    w1, w2, w2t, w1b, w2b, w2tb = state
    inner = first_w.shape[2]

    def one(member, head):
        return member[pl.ds(head, 1), :]

    def column(member, head):
        return jnp.broadcast_to(one(member, head), (TILE, HEAD)).T

    for c in range(count):
        head = jnp.minimum(me * count + c, total - 1) // (total // first_w.shape[0])
        row = one(first_b, head)
        fill = jnp.zeros((TILE - HEAD - 2, inner), F32)
        first = jnp.concatenate([first_w[head], row, row, fill], axis=0).T
        second_t = second_w[head]
        second = second_t.T
        w1[c] = first
        w1b[c] = split_bias(first)
        w2[c] = second
        w2b[c] = second.astype(BF16)
        w2t[c] = second_t
        w2tb[c] = second_t.astype(BF16)
        bias2[c] = column(second_b, head)
        gain[c] = column(norm_gain, head)
        shift[c] = column(norm_shift, head)


def rows_of(tile, chain, kind):
    chains, _, part = tile
    return chains[chain, part, kind * HEAD : (kind + 1) * HEAD, :]


def mini_batch(count, keys_low, learn, key_tile, query_tile, consts, state, bias2):
    gain, shift = consts
    w1, w2, w2t, w1b, w2b, w2tb = state
    each = range(count)
    lane = lax.broadcasted_iota(jnp.int32, (HEAD, TILE), 1)
    is_key = (lane < MB) if keys_low else (lane >= MB)
    row = lax.broadcasted_iota(jnp.int32, (HEAD, TILE), 0)
    ones_rows = jnp.where(row < 2, 1.0, 0.0)
    rows = [
        jnp.where(
            is_key,
            rows_of(key_tile, c, 1).astype(F32),
            rows_of(query_tile, c, 0).astype(F32),
        )
        for c in each
    ]
    wide = [jnp.concatenate([rows[c], ones_rows], axis=0).astype(BF16) for c in each]
    pre = [dot(w1b[c], wide[c]) for c in each]
    square = [p * p for p in pre]
    bend = [jnp.tanh((CURVE * p) * (1.0 + CUBIC * s)) for p, s in zip(pre, square)]
    half = [0.5 + 0.5 * t for t in bend]
    hidden = [(p * h).astype(BF16) for p, h in zip(pre, half)]
    outer = [dot(w2tb[c], hidden[c]) + bias2[c] for c in each]
    centered = [o - mean_rows(o) for o in outer]
    inverse = [lax.rsqrt(mean_rows(z * z) + 1e-06) for z in centered]
    normed = [z * i for z, i in zip(centered, inverse)]
    model = [gain[c] * normed[c] + shift[c] for c in each]
    answer = [rows[c] + model[c] for c in each]
    if not learn:
        return answer
    values = [rows_of(key_tile, c, 2).astype(F32) for c in each]
    upstream = [(model[c] - (values[c] - rows[c])) * gain[c] for c in each]
    grad_outer = [
        inverse[c]
        * (
            upstream[c]
            - mean_rows(upstream[c])
            - normed[c] * mean_rows(upstream[c] * normed[c])
        )
        for c in each
    ]
    rates = []
    pairs = key_tile[1][key_tile[2]].astype(F32)
    for c in each:
        rate = pairs[c : c + 1, :] + pairs[PAIRS + c : PAIRS + c + 1, :]
        rates.append(jnp.where(is_key[0:1, :], rate, 0.0))
    plain = [g.astype(BF16) for g in grad_outer]
    scaled_outer = [(rates[c] * grad_outer[c]).astype(BF16) for c in each]
    grad_hidden = [dot(w2b[c], plain[c]) for c in each]
    slope = [
        half[c]
        + (0.5 * CURVE) * pre[c] * (1.0 - bend[c] * bend[c]) * (1.0 + (3.0 * CUBIC) * square[c])
        for c in each
    ]
    scaled_inner = [(grad_hidden[c] * slope[c] * rates[c]).astype(BF16) for c in each]
    ones = jnp.ones((TILE, TILE), BF16)
    for c in each:
        new = w1[c] - dot(scaled_inner[c], wide[c], NT)
        w1[c] = new
        w1b[c] = split_bias(new)
    for c in each:
        new = w2t[c] - dot(scaled_outer[c], hidden[c], NT)
        w2t[c] = new
        w2tb[c] = new.astype(BF16)
        bias2[c] = bias2[c] - dot(scaled_outer[c], ones, NT)
        new = w2[c] - dot(hidden[c], scaled_outer[c], NT)
        w2[c] = new
        w2b[c] = new.astype(BF16)
    return answer


def flipped(index, bits, count):
    result = 0
    place = 1
    while place < count:
        bit = lax.rem(index // place, 2)
        result = result + place * ((1 - bit) if (bits // place) % 2 else bit)
        place *= 2
    return result


def partner(index, step, count):
    if count & (count - 1) == 0:
        return flipped(index, step, count)
    return lax.rem(index + step, count)


def greet(axes):
    barrier = pltpu.get_barrier_semaphore()
    for axis, count in axes:
        me = lax.axis_index(axis)
        for step in range(1, count):
            pl.semaphore_signal(
                barrier,
                inc=1,
                device_id={axis: lax.rem(me + step, count)},
                device_id_type=MESH,
            )
    pl.semaphore_wait(barrier, sum(count - 1 for _, count in axes))


def block_of(heads):
    return max(n for n in (4, 3, 2, 1) if heads % n == 0)


def project(sizes, group_me, mine, qkv, rate_weight, base, load, load_rates, weights, sums,
            land, weight_sem, token_send, token_recv, between, ready):
    places, group, seqs, heads, parts, count, own, pieces = sizes
    piece = mine.shape[2] // pieces
    total = seqs * heads
    block = group * own
    several = block_of(heads)

    def span(cut):
        return slice(cut * piece, (cut + 1) * piece)

    def fetch(cut):
        return pltpu.make_async_copy(
            qkv.at[:, span(cut)], weights.at[cut], weight_sem.at[cut]
        )

    def move(n, cut, step, peer, source):
        return pltpu.make_async_remote_copy(
            src_ref=mine.at[n, :, span(cut)],
            dst_ref=land.at[n, cut, source],
            send_sem=token_send.at[n, cut, step],
            recv_sem=token_recv.at[n, cut, source],
            device_id={"tensor": peer},
            device_id_type=MESH,
        )

    for n in range(seqs):
        for cut in range(pieces):
            for step in range(group - 1, 0, -1):
                move(n, cut, step, partner(group_me, step, group), group_me).start()
    for cut in range(pieces):
        fetch(cut).start()
    if places * count > total:
        load[...] = jnp.zeros_like(load)
    between()
    gates = []
    for n in range(seqs):
        logit = None
        for cut in range(pieces):
            land[n, cut, group_me] = mine[n, :, span(cut)]
            if n == 0:
                fetch(cut).wait()
            for step in range(group - 1, 0, -1):
                peer = partner(group_me, step, group)
                move(n, cut, step, peer, peer).wait_recv()
            tokens = land[n, cut].astype(F32).reshape(block, piece).astype(BF16)
            more = dot(rate_weight[:, span(cut)], tokens, NT)
            logit = more if logit is None else logit + more

            def some_heads(index, carry):
                start = pl.multiple_of(index * (several * 3 * HEAD), 64)
                rows = pl.ds(start, several * 3 * HEAD)
                part = dot(weights[cut, rows, :], tokens, NT)
                part = part.reshape(several, 3 * HEAD, block)
                at = pl.ds(index * several, several)
                sums[at] = part if cut == 0 else sums[at] + part
                return carry

            lax.fori_loop(0, heads // several, some_heads, 0)
        gates.append(jax.nn.sigmoid(logit))
        for head in range(heads):
            place, c = divmod(head * seqs + n, count)
            for part in range(parts):
                load[place, c, part] = sums[head, :, part * TILE : (part + 1) * TILE].astype(BF16)
        if n + 1 < seqs:
            ready(n)
    for place in range(places):
        for part in range(parts):
            coarse, fine = [], []
            for c in range(count):
                head, n = divmod(min(place * count + c, total - 1), seqs)
                row = base[head] * gates[n][head : head + 1, part * TILE : (part + 1) * TILE]
                short = row.astype(BF16).astype(F32)
                coarse.append(short)
                fine.append(row - short)
            fill = [jnp.zeros((PAIRS - count, TILE), F32)] if count < PAIRS else []
            load_rates[place, part] = jnp.concatenate(
                coarse + fill + fine + fill, axis=0
            ).astype(BF16)
    ready(seqs - 1)

    def drain():
        for n in range(seqs):
            for cut in range(pieces):
                for step in range(group - 1, 0, -1):
                    move(n, cut, step, partner(group_me, step, group), group_me).wait_send()

    return drain


def layer_kernel(sizes, mine, qkv, rate_weight, base, first_w, first_b, second_w, second_b,
                 norm_gain, norm_shift, mix_weight, out,
                 w1, w2, w2t, w1b, w2b, w2tb, bias2, low, gain, shift,
                 x, x_rates, arrive, arrive_rates, outs, back, weights, sums, land, mix, ready, shares,
                 weight_sem, token_send, token_recv, mix_sem,
                 send_sem, recv_sem, own_sem, back_send, back_recv, back_own,
                 share_send, share_recv):
    places, group, seqs, heads, parts, count, own_rows, pieces = sizes
    total_chains = seqs * heads
    me = lax.axis_index("seq")
    group_me = lax.axis_index("tensor")
    greet((("tensor", group), ("seq", places)))

    def forward(step, c, peer, source):
        return pltpu.make_async_remote_copy(
            src_ref=x.at[peer, c],
            dst_ref=arrive.at[source, c],
            send_sem=send_sem.at[step, c],
            recv_sem=recv_sem.at[source, c],
            device_id={"seq": peer},
            device_id_type=MESH,
        )

    def forward_rates(step, peer, source):
        return pltpu.make_async_remote_copy(
            src_ref=x_rates.at[peer],
            dst_ref=arrive_rates.at[source],
            send_sem=send_sem.at[step, count],
            recv_sem=recv_sem.at[source, count],
            device_id={"seq": peer},
            device_id_type=MESH,
        )

    def homeward(place, source):
        return pltpu.make_async_remote_copy(
            src_ref=outs.at[place],
            dst_ref=back.at[source],
            send_sem=back_send.at[place],
            recv_sem=back_recv.at[source],
            device_id={"seq": place},
            device_id_type=MESH,
        )

    own = pltpu.make_async_copy(x.at[me], arrive.at[me], own_sem.at[0])
    own_rates = pltpu.make_async_copy(x_rates.at[me], arrive_rates.at[me], own_sem.at[1])
    own_back = pltpu.make_async_copy(outs.at[me], back.at[me], back_own)
    mix_copy = pltpu.make_async_copy(mix_weight, mix, mix_sem)
    state = (w1, w2, w2t, w1b, w2b, w2tb)
    consts = (gain, shift)
    params = (first_w, first_b, second_w, second_b, norm_gain, norm_shift)

    def between():
        mix_copy.start()
        load_state(me, count, total_chains, params, consts, state, bias2)
        low[...] = jnp.zeros_like(low)

    def ready_rows(n):
        if n == seqs - 1:
            for step in range(places - 1, 0, -1):
                forward_rates(step, partner(me, step, places), me).start()
            own.start()
            own_rates.start()
        for step in range(places - 1, 0, -1):
            peer = partner(me, step, places)
            for c in range(count):

                @pl.when(lax.rem(peer * count + c, seqs) == n)
                def _():
                    forward(step, c, peer, me).start()

    drain = project(
        sizes, group_me, mine, qkv, rate_weight, base, x, x_rates, weights, sums, land,
        weight_sem, token_send, token_recv, between, ready_rows,
    )
    lane = lax.broadcasted_iota(jnp.int32, (HEAD, TILE), 1)

    def finish(place, part, answer):
        for c in range(count):
            outs[place, part, c * HEAD : (c + 1) * HEAD, :] = jnp.where(
                lane < MB, low[c], answer[c]
            ).astype(BF16)

    def send_home(place):
        @pl.when(place == me)
        def _():
            own_back.start()

        @pl.when(place != me)
        def _():
            homeward(place, me).start()

    def body(place, carry):
        @pl.when(place == me)
        def _():
            own.wait()
            own_rates.wait()

        @pl.when(place != me)
        def _():
            forward_rates(0, place, place).wait_recv()
            for c in range(count):
                forward(0, c, place, place).wait_recv()

        for part in range(parts):
            tile = (arrive.at[place], arrive_rates.at[place], part)
            if part:
                old_place, old_part = place, part - 1
            else:
                old_place, old_part = jnp.maximum(place - 1, 0), parts - 1
            before = (arrive.at[old_place], None, old_part)
            answer = mini_batch(count, True, True, tile, before, consts, state, bias2)
            finish(old_place, old_part, answer)
            if not part:

                @pl.when(place > 0)
                def _():
                    send_home(place - 1)

            answer = mini_batch(count, False, True, tile, tile, consts, state, bias2)
            for c in range(count):
                low[c] = answer[c]
        return carry

    lax.fori_loop(0, places, body, 0)
    last = (arrive.at[places - 1], None, parts - 1)
    answer = mini_batch(count, True, False, last, last, consts, state, bias2)
    finish(places - 1, parts - 1, answer)
    send_home(places - 1)
    own_back.wait()
    for step in range(1, places):
        peer = partner(me, step, places)
        forward_rates(step, peer, me).wait_send()
        for c in range(count):
            forward(step, c, peer, me).wait_send()
        homeward(peer, peer).wait_recv()
        homeward(peer, me).wait_send()


    mix_copy.wait()

    def heads_of(n):
        tiles = []
        for part in range(parts):
            found = []
            for head in range(heads):
                place, c = divmod(head * seqs + n, count)
                found.append(back[place, part, c * HEAD : (c + 1) * HEAD, :].astype(F32))
            tiles.append(jnp.concatenate(found, axis=0).T)
        return jnp.concatenate(tiles, axis=0).astype(BF16)

    rows = [heads_of(n) for n in range(seqs)]
    width = mix.shape[1]
    cuts = ready.shape[0]
    piece = width // cuts

    def move(cut, step, peer):
        return pltpu.make_async_remote_copy(
            src_ref=ready.at[cut, peer],
            dst_ref=shares.at[cut, step],
            send_sem=share_send.at[cut, step],
            recv_sem=share_recv.at[cut, step],
            device_id={"tensor": peer},
            device_id_type=MESH,
        )

    both = jnp.concatenate(rows, axis=0)
    for cut in range(cuts):
        part = dot(both, mix[:, cut * piece : (cut + 1) * piece])
        part = part.reshape(seqs, group, own_rows, piece)
        ready[cut] = jnp.concatenate([part[n] for n in range(seqs)], axis=1).astype(BF16)
        for step in range(group - 1, 0, -1):
            move(cut, step, partner(group_me, step, group)).start()
    for cut in range(cuts):
        result = ready[cut, group_me].astype(F32)
        for step in range(group - 1, 0, -1):
            move(cut, step, partner(group_me, step, group)).wait_recv()
            result = result + shares[cut, step].astype(F32)
        out[:, cut * piece : (cut + 1) * piece] = result.astype(BF16)
    for cut in range(cuts):
        for step in range(group - 1, 0, -1):
            move(cut, step, partner(group_me, step, group)).wait_send()
    drain()


def shards(
    tokens,
    qkv_weight,
    rate_weight,
    base_rate,
    first_w,
    first_b,
    second_w,
    second_b,
    norm_gain,
    norm_shift,
    out_weight,
):
    places = lax.axis_size("seq")
    group = lax.axis_size("tensor")
    seqs, own, width = tokens.shape
    block = own * group
    heads, _, inner = first_w.shape
    assert block % TILE == 0
    parts = block // TILE
    count = -(-seqs * heads // places)
    assert count <= PAIRS
    pieces = cuts = 6
    piece = width // pieces
    sizes = (places, group, seqs, heads, parts, count, own, pieces)
    vmem = pl.BlockSpec(memory_space=pltpu.VMEM)
    whole = pl.BlockSpec(memory_space=pl.ANY)
    dma = pltpu.SemaphoreType.DMA
    out = pl.pallas_call(
        functools.partial(layer_kernel, sizes),
        out_shape=jax.ShapeDtypeStruct((seqs * own, width), BF16),
        in_specs=[vmem, whole, vmem, pl.BlockSpec(memory_space=pltpu.SMEM)] + [vmem] * 6 + [whole],
        out_specs=vmem,
        scratch_shapes=[
            pltpu.VMEM((count, inner, TILE), F32),
            pltpu.VMEM((count, inner, HEAD), F32),
            pltpu.VMEM((count, HEAD, inner), F32),
            pltpu.VMEM((count, inner, TILE), BF16),
            pltpu.VMEM((count, inner, HEAD), BF16),
            pltpu.VMEM((count, HEAD, inner), BF16),
            pltpu.VMEM((count, HEAD, TILE), F32),
            pltpu.VMEM((count, HEAD, TILE), F32),
            pltpu.VMEM((count, HEAD, TILE), F32),
            pltpu.VMEM((count, HEAD, TILE), F32),
            pltpu.VMEM((places, count, parts, 3 * HEAD, TILE), BF16),
            pltpu.VMEM((places, parts, 2 * PAIRS, TILE), BF16),
            pltpu.VMEM((places, count, parts, 3 * HEAD, TILE), BF16),
            pltpu.VMEM((places, parts, 2 * PAIRS, TILE), BF16),
            pltpu.VMEM((places, parts, count * HEAD, TILE), BF16),
            pltpu.VMEM((places, parts, count * HEAD, TILE), BF16),
            pltpu.VMEM((pieces, heads * 3 * HEAD, piece), BF16),
            pltpu.VMEM((heads, 3 * HEAD, block), F32),
            pltpu.VMEM((seqs, pieces, group, own, piece), BF16),
            pltpu.VMEM((heads * HEAD, width), BF16),
            pltpu.VMEM((cuts, group, seqs * own, width // cuts), BF16),
            pltpu.VMEM((cuts, group, seqs * own, width // cuts), BF16),
            dma((pieces,)),
            dma((seqs, pieces, group)),
            dma((seqs, pieces, group)),
            dma,
            dma((places, count + 1)),
            dma((places, count + 1)),
            dma((2,)),
            dma((places,)),
            dma((places,)),
            dma,
            dma((cuts, group)),
            dma((cuts, group)),
        ],
        compiler_params=pltpu.CompilerParams(
            collective_id=1, has_side_effects=True, vmem_limit_bytes=56 * 1024 * 1024
        ),
    )(
        tokens,
        qkv_weight.reshape(-1, width),
        rate_weight,
        base_rate,
        first_w,
        first_b,
        jnp.swapaxes(second_w, 1, 2),
        second_b,
        norm_gain,
        norm_shift,
        out_weight,
    )
    return out.reshape(tokens.shape)


def solution(mesh):
    in_specs = (
        P(None, ("seq", "tensor"), None),
        P("tensor", None, None),
        P("tensor", None),
        P("tensor"),
        P("tensor", None, None),
        P("tensor", None),
        P("tensor", None, None),
        P("tensor", None),
        P("tensor", None),
        P("tensor", None),
        P("tensor", None),
    )
    out_specs = P(None, ("seq", "tensor"), None)
    return jax.shard_map(shards, mesh=mesh, in_specs=in_specs, out_specs=out_specs, check_vma=False)
```

```python
import functools
import math

import jax
import jax.numpy as jnp
from jax import lax
from jax.experimental import pallas as pl
from jax.experimental.pallas import tpu as pltpu
from jax.sharding import PartitionSpec as P

HEAD = 64
MB = 64
TILE = 128
PAIRS = 8
CURVE = math.sqrt(2.0 / math.pi)
CUBIC = 0.044715
F32 = jnp.float32
BF16 = jnp.bfloat16
MESH = pl.DeviceIdType.MESH
NN = (((1,), (0,)), ((), ()))
NT = (((1,), (1,)), ((), ()))


def dot(a, b, dims=NN):
    return lax.dot_general(a, b, dims, preferred_element_type=F32)


def split_bias(state):
    lane = lax.broadcasted_iota(jnp.int32, state.shape, 1)
    rest = state - state.astype(BF16).astype(F32)
    return jnp.where(lane == HEAD + 1, rest, state).astype(BF16)


def mean_rows(values):
    return jnp.sum(values, axis=0, keepdims=True) * (1.0 / HEAD)


def load_state(me, count, total, params, consts, state, bias2):
    first_w, first_b, second_w, second_b, norm_gain, norm_shift = params
    gain, shift = consts
    w1, w2, w2t, w1b, w2b, w2tb = state
    inner = first_w.shape[2]

    def one(member, head):
        return member[pl.ds(head, 1), :]

    def column(member, head):
        return jnp.broadcast_to(one(member, head), (TILE, HEAD)).T

    for c in range(count):
        head = jnp.minimum(me * count + c, total - 1) // (total // first_w.shape[0])
        row = one(first_b, head)
        fill = jnp.zeros((TILE - HEAD - 2, inner), F32)
        first = jnp.concatenate([first_w[head], row, row, fill], axis=0).T
        second_t = second_w[head]
        second = second_t.T
        w1[c] = first
        w1b[c] = split_bias(first)
        w2[c] = second
        w2b[c] = second.astype(BF16)
        w2t[c] = second_t
        w2tb[c] = second_t.astype(BF16)
        bias2[c] = column(second_b, head)
        gain[c] = column(norm_gain, head)
        shift[c] = column(norm_shift, head)


def rows_of(tile, chain, kind):
    chains, _, part = tile
    return chains[chain, part, kind * HEAD : (kind + 1) * HEAD, :]


def mini_batch(count, keys_low, learn, key_tile, query_tile, consts, state, bias2):
    gain, shift = consts
    w1, w2, w2t, w1b, w2b, w2tb = state
    each = range(count)
    lane = lax.broadcasted_iota(jnp.int32, (HEAD, TILE), 1)
    is_key = (lane < MB) if keys_low else (lane >= MB)
    row = lax.broadcasted_iota(jnp.int32, (HEAD, TILE), 0)
    ones_rows = jnp.where(row < 2, 1.0, 0.0)
    rows = [
        jnp.where(
            is_key,
            rows_of(key_tile, c, 1).astype(F32),
            rows_of(query_tile, c, 0).astype(F32),
        )
        for c in each
    ]
    wide = [jnp.concatenate([rows[c], ones_rows], axis=0).astype(BF16) for c in each]
    pre = [dot(w1b[c], wide[c]) for c in each]
    square = [p * p for p in pre]
    bend = [jnp.tanh((CURVE * p) * (1.0 + CUBIC * s)) for p, s in zip(pre, square)]
    half = [0.5 + 0.5 * t for t in bend]
    hidden = [(p * h).astype(BF16) for p, h in zip(pre, half)]
    outer = [dot(w2tb[c], hidden[c]) + bias2[c] for c in each]
    centered = [o - mean_rows(o) for o in outer]
    inverse = [lax.rsqrt(mean_rows(z * z) + 1e-06) for z in centered]
    normed = [z * i for z, i in zip(centered, inverse)]
    model = [gain[c] * normed[c] + shift[c] for c in each]
    answer = [rows[c] + model[c] for c in each]
    if not learn:
        return answer
    values = [rows_of(key_tile, c, 2).astype(F32) for c in each]
    upstream = [(model[c] - (values[c] - rows[c])) * gain[c] for c in each]
    grad_outer = [
        inverse[c]
        * (
            upstream[c]
            - mean_rows(upstream[c])
            - normed[c] * mean_rows(upstream[c] * normed[c])
        )
        for c in each
    ]
    rates = []
    pairs = key_tile[1][key_tile[2]].astype(F32)
    for c in each:
        rate = pairs[c : c + 1, :] + pairs[PAIRS + c : PAIRS + c + 1, :]
        rates.append(jnp.where(is_key[0:1, :], rate, 0.0))
    plain = [g.astype(BF16) for g in grad_outer]
    scaled_outer = [(rates[c] * grad_outer[c]).astype(BF16) for c in each]
    grad_hidden = [dot(w2b[c], plain[c]) for c in each]
    slope = [
        half[c]
        + (0.5 * CURVE) * pre[c] * (1.0 - bend[c] * bend[c]) * (1.0 + (3.0 * CUBIC) * square[c])
        for c in each
    ]
    scaled_inner = [(grad_hidden[c] * slope[c] * rates[c]).astype(BF16) for c in each]
    ones = jnp.ones((TILE, TILE), BF16)
    for c in each:
        new = w1[c] - dot(scaled_inner[c], wide[c], NT)
        w1[c] = new
        w1b[c] = split_bias(new)
    for c in each:
        new = w2t[c] - dot(scaled_outer[c], hidden[c], NT)
        w2t[c] = new
        w2tb[c] = new.astype(BF16)
        bias2[c] = bias2[c] - dot(scaled_outer[c], ones, NT)
        new = w2[c] - dot(hidden[c], scaled_outer[c], NT)
        w2[c] = new
        w2b[c] = new.astype(BF16)
    return answer


def flipped(index, bits, count):
    result = 0
    place = 1
    while place < count:
        bit = lax.rem(index // place, 2)
        result = result + place * ((1 - bit) if (bits // place) % 2 else bit)
        place *= 2
    return result


def partner(index, step, count):
    if count & (count - 1) == 0:
        return flipped(index, step, count)
    return lax.rem(index + step, count)


def greet(axes):
    barrier = pltpu.get_barrier_semaphore()
    for axis, count in axes:
        me = lax.axis_index(axis)
        for step in range(1, count):
            pl.semaphore_signal(
                barrier,
                inc=1,
                device_id={axis: lax.rem(me + step, count)},
                device_id_type=MESH,
            )
    pl.semaphore_wait(barrier, sum(count - 1 for _, count in axes))


def block_of(heads):
    return max(n for n in (4, 3, 2, 1) if heads % n == 0)


def project(sizes, group_me, mine, qkv, rate_weight, base, load, load_rates, weights, sums,
            land, weight_sem, token_send, token_recv, between, ready):
    places, group, seqs, heads, parts, count, own, pieces = sizes
    piece = mine.shape[2] // pieces
    total = seqs * heads
    block = group * own
    several = block_of(heads)

    def span(cut):
        return slice(cut * piece, (cut + 1) * piece)

    def fetch(cut):
        return pltpu.make_async_copy(
            qkv.at[:, span(cut)], weights.at[cut], weight_sem.at[cut]
        )

    def move(n, cut, step, peer, source):
        return pltpu.make_async_remote_copy(
            src_ref=mine.at[n, :, span(cut)],
            dst_ref=land.at[n, cut, source],
            send_sem=token_send.at[n, cut, step],
            recv_sem=token_recv.at[n, cut, source],
            device_id={"tensor": peer},
            device_id_type=MESH,
        )

    square = group == 4
    direct = (2, 1) if square else tuple(range(group - 1, 0, -1))

    def relay(n, cut):
        held, across = ((1, 2), (2, 1))[cut % 2]
        source = partner(group_me, held, group)
        return pltpu.make_async_remote_copy(
            src_ref=land.at[n, cut, source],
            dst_ref=land.at[n, cut, source],
            send_sem=token_send.at[n, cut, 3],
            recv_sem=token_recv.at[n, cut, source],
            device_id={"tensor": partner(group_me, across, group)},
            device_id_type=MESH,
        )

    def receive(n, cut):
        for step in direct:
            peer = partner(group_me, step, group)
            move(n, cut, step, peer, peer).wait_recv()
        if square:
            relay(n, cut).start()

    for n in range(seqs):
        for cut in range(pieces):
            for step in direct:
                move(n, cut, step, partner(group_me, step, group), group_me).start()
    for cut in range(pieces):
        fetch(cut).start()
    if places * count > total:
        load[...] = jnp.zeros_like(load)
    between()
    gates = []
    order = [(n, cut) for n in range(seqs) for cut in range(pieces)]
    receive(0, 0)
    for n in range(seqs):
        logit = None
        for cut in range(pieces):
            land[n, cut, group_me] = mine[n, :, span(cut)]
            if n == 0:
                fetch(cut).wait()
            at = order.index((n, cut)) + 1
            if at < len(order):
                receive(*order[at])
            if square:
                peer = partner(group_me, 3, group)
                move(n, cut, 3, peer, peer).wait_recv()
            tokens = land[n, cut].astype(F32).reshape(block, piece).astype(BF16)
            more = dot(rate_weight[:, span(cut)], tokens, NT)
            logit = more if logit is None else logit + more

            def some_heads(index, carry):
                start = pl.multiple_of(index * (several * 3 * HEAD), 64)
                rows = pl.ds(start, several * 3 * HEAD)
                part = dot(weights[cut, rows, :], tokens, NT)
                part = part.reshape(several, 3 * HEAD, block)
                at = pl.ds(index * several, several)
                sums[at] = part if cut == 0 else sums[at] + part
                return carry

            lax.fori_loop(0, heads // several, some_heads, 0)
        gates.append(jax.nn.sigmoid(logit))
        for head in range(heads):
            place, c = divmod(head * seqs + n, count)
            for part in range(parts):
                load[place, c, part] = sums[head, :, part * TILE : (part + 1) * TILE].astype(BF16)
        if n + 1 < seqs:
            ready(n)
    for place in range(places):
        for part in range(parts):
            coarse, fine = [], []
            for c in range(count):
                head, n = divmod(min(place * count + c, total - 1), seqs)
                row = base[head] * gates[n][head : head + 1, part * TILE : (part + 1) * TILE]
                short = row.astype(BF16).astype(F32)
                coarse.append(short)
                fine.append(row - short)
            fill = [jnp.zeros((PAIRS - count, TILE), F32)] if count < PAIRS else []
            load_rates[place, part] = jnp.concatenate(
                coarse + fill + fine + fill, axis=0
            ).astype(BF16)
    ready(seqs - 1)

    def drain():
        for n in range(seqs):
            for cut in range(pieces):
                for step in direct:
                    move(n, cut, step, partner(group_me, step, group), group_me).wait_send()
                if square:
                    relay(n, cut).wait_send()

    return drain


def layer_kernel(sizes, mine, qkv, rate_weight, base, first_w, first_b, second_w, second_b,
                 norm_gain, norm_shift, mix_weight, out,
                 w1, w2, w2t, w1b, w2b, w2tb, bias2, low, gain, shift,
                 x, x_rates, arrive, arrive_rates, outs, back, weights, sums, land, mix, ready, shares,
                 weight_sem, token_send, token_recv, mix_sem,
                 send_sem, recv_sem, own_sem, back_send, back_recv, back_own,
                 share_send, share_recv):
    places, group, seqs, heads, parts, count, own_rows, pieces = sizes
    total_chains = seqs * heads
    me = lax.axis_index("seq")
    group_me = lax.axis_index("tensor")
    greet((("tensor", group), ("seq", places)))

    def forward(step, c, peer, source):
        return pltpu.make_async_remote_copy(
            src_ref=x.at[peer, c],
            dst_ref=arrive.at[source, c],
            send_sem=send_sem.at[step, c],
            recv_sem=recv_sem.at[source, c],
            device_id={"seq": peer},
            device_id_type=MESH,
        )

    def forward_rates(step, peer, source):
        return pltpu.make_async_remote_copy(
            src_ref=x_rates.at[peer],
            dst_ref=arrive_rates.at[source],
            send_sem=send_sem.at[step, count],
            recv_sem=recv_sem.at[source, count],
            device_id={"seq": peer},
            device_id_type=MESH,
        )

    def homeward(place, source):
        return pltpu.make_async_remote_copy(
            src_ref=outs.at[place],
            dst_ref=back.at[source],
            send_sem=back_send.at[place],
            recv_sem=back_recv.at[source],
            device_id={"seq": place},
            device_id_type=MESH,
        )

    own = pltpu.make_async_copy(x.at[me], arrive.at[me], own_sem.at[0])
    own_rates = pltpu.make_async_copy(x_rates.at[me], arrive_rates.at[me], own_sem.at[1])
    own_back = pltpu.make_async_copy(outs.at[me], back.at[me], back_own)
    mix_copy = pltpu.make_async_copy(mix_weight, mix, mix_sem)
    state = (w1, w2, w2t, w1b, w2b, w2tb)
    consts = (gain, shift)
    params = (first_w, first_b, second_w, second_b, norm_gain, norm_shift)

    def between():
        mix_copy.start()
        load_state(me, count, total_chains, params, consts, state, bias2)
        low[...] = jnp.zeros_like(low)

    def ready_rows(n):
        if n == seqs - 1:
            for step in range(places - 1, 0, -1):
                forward_rates(step, partner(me, step, places), me).start()
            own.start()
            own_rates.start()
        for step in range(places - 1, 0, -1):
            peer = partner(me, step, places)
            for c in range(count):

                @pl.when(lax.rem(peer * count + c, seqs) == n)
                def _():
                    forward(step, c, peer, me).start()

    drain = project(
        sizes, group_me, mine, qkv, rate_weight, base, x, x_rates, weights, sums, land,
        weight_sem, token_send, token_recv, between, ready_rows,
    )
    lane = lax.broadcasted_iota(jnp.int32, (HEAD, TILE), 1)

    def finish(place, part, answer):
        for c in range(count):
            outs[place, part, c * HEAD : (c + 1) * HEAD, :] = jnp.where(
                lane < MB, low[c], answer[c]
            ).astype(BF16)

    def send_home(place):
        @pl.when(place == me)
        def _():
            own_back.start()

        @pl.when(place != me)
        def _():
            homeward(place, me).start()

    def body(place, carry):
        @pl.when(place == me)
        def _():
            own.wait()
            own_rates.wait()

        @pl.when(place != me)
        def _():
            forward_rates(0, place, place).wait_recv()
            for c in range(count):
                forward(0, c, place, place).wait_recv()

        for part in range(parts):
            tile = (arrive.at[place], arrive_rates.at[place], part)
            if part:
                old_place, old_part = place, part - 1
            else:
                old_place, old_part = jnp.maximum(place - 1, 0), parts - 1
            before = (arrive.at[old_place], None, old_part)
            answer = mini_batch(count, True, True, tile, before, consts, state, bias2)
            finish(old_place, old_part, answer)
            if not part:

                @pl.when(place > 0)
                def _():
                    send_home(place - 1)

            answer = mini_batch(count, False, True, tile, tile, consts, state, bias2)
            for c in range(count):
                low[c] = answer[c]
        return carry

    lax.fori_loop(0, places, body, 0)
    last = (arrive.at[places - 1], None, parts - 1)
    answer = mini_batch(count, True, False, last, last, consts, state, bias2)
    finish(places - 1, parts - 1, answer)
    send_home(places - 1)
    own_back.wait()
    for step in range(1, places):
        peer = partner(me, step, places)
        forward_rates(step, peer, me).wait_send()
        for c in range(count):
            forward(step, c, peer, me).wait_send()
        homeward(peer, peer).wait_recv()
        homeward(peer, me).wait_send()


    mix_copy.wait()

    def heads_of(n):
        tiles = []
        for part in range(parts):
            found = []
            for head in range(heads):
                place, c = divmod(head * seqs + n, count)
                found.append(back[place, part, c * HEAD : (c + 1) * HEAD, :].astype(F32))
            tiles.append(jnp.concatenate(found, axis=0).T)
        return jnp.concatenate(tiles, axis=0).astype(BF16)

    rows = [heads_of(n) for n in range(seqs)]
    width = mix.shape[1]
    cuts = ready.shape[0]
    piece = width // cuts

    def move(cut, row, slot, step):
        peer = partner(group_me, step, group)
        return pltpu.make_async_remote_copy(
            src_ref=ready.at[cut, partner(group_me, row, group)],
            dst_ref=shares.at[cut, slot],
            send_sem=share_send.at[cut, slot],
            recv_sem=share_recv.at[cut, slot],
            device_id={"tensor": peer},
            device_id_type=MESH,
        )

    def sends(cut):
        if group != 4:
            return [(step, step, step) for step in range(group - 1, 0, -1)], None
        near, far = ((1, 2), (2, 1))[cut % 2]
        return [(3, 3, near), (near, near, near)], (far, far, far)

    def pass_on(cut):
        first, later = sends(cut)
        if later is None:
            return
        move(cut, *first[0]).wait_recv()
        row = partner(group_me, later[0], group)
        joint = ready[cut, row].astype(F32) + shares[cut, 3].astype(F32)
        ready[cut, row] = joint.astype(BF16)
        move(cut, *later).start()

    both = jnp.concatenate(rows, axis=0)
    for cut in range(cuts):
        part = dot(both, mix[:, cut * piece : (cut + 1) * piece])
        part = part.reshape(seqs, group, own_rows, piece)
        ready[cut] = jnp.concatenate([part[n] for n in range(seqs)], axis=1).astype(BF16)
        for each in sends(cut)[0]:
            move(cut, *each).start()
        if cut >= 2:
            pass_on(cut - 2)
    for cut in range(cuts - 2, cuts):
        pass_on(cut)
    for cut in range(cuts):
        result = ready[cut, group_me].astype(F32)
        first, later = sends(cut)
        ends = first if later is None else [first[1], later]
        for each in ends:
            move(cut, *each).wait_recv()
            result = result + shares[cut, each[1]].astype(F32)
        out[:, cut * piece : (cut + 1) * piece] = result.astype(BF16)
    for cut in range(cuts):
        first, later = sends(cut)
        for each in first + ([] if later is None else [later]):
            move(cut, *each).wait_send()
    drain()


def shards(
    tokens,
    qkv_weight,
    rate_weight,
    base_rate,
    first_w,
    first_b,
    second_w,
    second_b,
    norm_gain,
    norm_shift,
    out_weight,
):
    places = lax.axis_size("seq")
    group = lax.axis_size("tensor")
    seqs, own, width = tokens.shape
    block = own * group
    heads, _, inner = first_w.shape
    assert block % TILE == 0
    parts = block // TILE
    count = -(-seqs * heads // places)
    assert count <= PAIRS
    pieces = cuts = 6
    piece = width // pieces
    sizes = (places, group, seqs, heads, parts, count, own, pieces)
    vmem = pl.BlockSpec(memory_space=pltpu.VMEM)
    whole = pl.BlockSpec(memory_space=pl.ANY)
    dma = pltpu.SemaphoreType.DMA
    out = pl.pallas_call(
        functools.partial(layer_kernel, sizes),
        out_shape=jax.ShapeDtypeStruct((seqs * own, width), BF16),
        in_specs=[vmem, whole, vmem, pl.BlockSpec(memory_space=pltpu.SMEM)] + [vmem] * 6 + [whole],
        out_specs=vmem,
        scratch_shapes=[
            pltpu.VMEM((count, inner, TILE), F32),
            pltpu.VMEM((count, inner, HEAD), F32),
            pltpu.VMEM((count, HEAD, inner), F32),
            pltpu.VMEM((count, inner, TILE), BF16),
            pltpu.VMEM((count, inner, HEAD), BF16),
            pltpu.VMEM((count, HEAD, inner), BF16),
            pltpu.VMEM((count, HEAD, TILE), F32),
            pltpu.VMEM((count, HEAD, TILE), F32),
            pltpu.VMEM((count, HEAD, TILE), F32),
            pltpu.VMEM((count, HEAD, TILE), F32),
            pltpu.VMEM((places, count, parts, 3 * HEAD, TILE), BF16),
            pltpu.VMEM((places, parts, 2 * PAIRS, TILE), BF16),
            pltpu.VMEM((places, count, parts, 3 * HEAD, TILE), BF16),
            pltpu.VMEM((places, parts, 2 * PAIRS, TILE), BF16),
            pltpu.VMEM((places, parts, count * HEAD, TILE), BF16),
            pltpu.VMEM((places, parts, count * HEAD, TILE), BF16),
            pltpu.VMEM((pieces, heads * 3 * HEAD, piece), BF16),
            pltpu.VMEM((heads, 3 * HEAD, block), F32),
            pltpu.VMEM((seqs, pieces, group, own, piece), BF16),
            pltpu.VMEM((heads * HEAD, width), BF16),
            pltpu.VMEM((cuts, group, seqs * own, width // cuts), BF16),
            pltpu.VMEM((cuts, group, seqs * own, width // cuts), BF16),
            dma((pieces,)),
            dma((seqs, pieces, group)),
            dma((seqs, pieces, group)),
            dma,
            dma((places, count + 1)),
            dma((places, count + 1)),
            dma((2,)),
            dma((places,)),
            dma((places,)),
            dma,
            dma((cuts, group)),
            dma((cuts, group)),
        ],
        compiler_params=pltpu.CompilerParams(
            collective_id=1, has_side_effects=True, vmem_limit_bytes=56 * 1024 * 1024
        ),
    )(
        tokens,
        qkv_weight.reshape(-1, width),
        rate_weight,
        base_rate,
        first_w,
        first_b,
        jnp.swapaxes(second_w, 1, 2),
        second_b,
        norm_gain,
        norm_shift,
        out_weight,
    )
    return out.reshape(tokens.shape)


def solution(mesh):
    in_specs = (
        P(None, ("seq", "tensor"), None),
        P("tensor", None, None),
        P("tensor", None),
        P("tensor"),
        P("tensor", None, None),
        P("tensor", None),
        P("tensor", None, None),
        P("tensor", None),
        P("tensor", None),
        P("tensor", None),
        P("tensor", None),
    )
    out_specs = P(None, ("seq", "tensor"), None)
    return jax.shard_map(shards, mesh=mesh, in_specs=in_specs, out_specs=out_specs, check_vma=False)
```

```python
import functools
import math

import jax
import jax.numpy as jnp
from jax import lax
from jax.experimental import pallas as pl
from jax.experimental.pallas import tpu as pltpu
from jax.sharding import PartitionSpec as P

HEAD = 64
MB = 64
TILE = 128
PAIRS = 8
CURVE = math.sqrt(2.0 / math.pi)
CUBIC = 0.044715
F32 = jnp.float32
BF16 = jnp.bfloat16
MESH = pl.DeviceIdType.MESH
NN = (((1,), (0,)), ((), ()))
NT = (((1,), (1,)), ((), ()))


def dot(a, b, dims=NN):
    return lax.dot_general(a, b, dims, preferred_element_type=F32)


def split_bias(state):
    lane = lax.broadcasted_iota(jnp.int32, state.shape, 1)
    rest = state - state.astype(BF16).astype(F32)
    return jnp.where(lane == HEAD + 1, rest, state).astype(BF16)


def mean_rows(values):
    return jnp.sum(values, axis=0, keepdims=True) * (1.0 / HEAD)


def load_state(me, count, total, params, consts, state, bias2):
    first_w, first_b, second_w, second_b, norm_gain, norm_shift = params
    gain, shift = consts
    w1, w2, w2t, w1b, w2b, w2tb = state
    inner = first_w.shape[2]

    def one(member, head):
        return member[pl.ds(head, 1), :]

    def column(member, head):
        return jnp.broadcast_to(one(member, head), (TILE, HEAD)).T

    for c in range(count):
        head = jnp.minimum(me * count + c, total - 1) // (total // first_w.shape[0])
        row = one(first_b, head)
        fill = jnp.zeros((TILE - HEAD - 2, inner), F32)
        first = jnp.concatenate([first_w[head], row, row, fill], axis=0).T
        second_t = second_w[head]
        second = second_t.T
        w1[c] = first
        w1b[c] = split_bias(first)
        w2[c] = second
        w2b[c] = second.astype(BF16)
        w2t[c] = second_t
        w2tb[c] = second_t.astype(BF16)
        bias2[c] = column(second_b, head)
        gain[c] = column(norm_gain, head)
        shift[c] = column(norm_shift, head)


def rows_of(tile, chain, kind):
    chains, _, part = tile
    return chains[chain, part, kind * HEAD : (kind + 1) * HEAD, :]


def mini_batch(count, keys_low, learn, key_tile, query_tile, consts, state, bias2):
    gain, shift = consts
    w1, w2, w2t, w1b, w2b, w2tb = state
    each = range(count)
    lane = lax.broadcasted_iota(jnp.int32, (HEAD, TILE), 1)
    is_key = (lane < MB) if keys_low else (lane >= MB)
    row = lax.broadcasted_iota(jnp.int32, (HEAD, TILE), 0)
    ones_rows = jnp.where(row < 2, 1.0, 0.0)
    rows = [
        jnp.where(
            is_key,
            rows_of(key_tile, c, 1).astype(F32),
            rows_of(query_tile, c, 0).astype(F32),
        )
        for c in each
    ]
    wide = [jnp.concatenate([rows[c], ones_rows], axis=0).astype(BF16) for c in each]
    pre = [dot(w1b[c], wide[c]) for c in each]
    square = [p * p for p in pre]
    bend = [jnp.tanh((CURVE * p) * (1.0 + CUBIC * s)) for p, s in zip(pre, square)]
    half = [0.5 + 0.5 * t for t in bend]
    hidden = [(p * h).astype(BF16) for p, h in zip(pre, half)]
    outer = [dot(w2tb[c], hidden[c]) + bias2[c] for c in each]
    centered = [o - mean_rows(o) for o in outer]
    inverse = [lax.rsqrt(mean_rows(z * z) + 1e-06) for z in centered]
    normed = [z * i for z, i in zip(centered, inverse)]
    model = [gain[c] * normed[c] + shift[c] for c in each]
    answer = [rows[c] + model[c] for c in each]
    if not learn:
        return answer
    values = [rows_of(key_tile, c, 2).astype(F32) for c in each]
    upstream = [(model[c] - (values[c] - rows[c])) * gain[c] for c in each]
    grad_outer = [
        inverse[c]
        * (
            upstream[c]
            - mean_rows(upstream[c])
            - normed[c] * mean_rows(upstream[c] * normed[c])
        )
        for c in each
    ]
    rates = []
    pairs = key_tile[1][key_tile[2]].astype(F32)
    for c in each:
        rate = pairs[c : c + 1, :] + pairs[PAIRS + c : PAIRS + c + 1, :]
        rates.append(jnp.where(is_key[0:1, :], rate, 0.0))
    plain = [g.astype(BF16) for g in grad_outer]
    scaled_outer = [(rates[c] * grad_outer[c]).astype(BF16) for c in each]
    grad_hidden = [dot(w2b[c], plain[c]) for c in each]
    slope = [
        half[c]
        + (0.5 * CURVE) * pre[c] * (1.0 - bend[c] * bend[c]) * (1.0 + (3.0 * CUBIC) * square[c])
        for c in each
    ]
    scaled_inner = [(grad_hidden[c] * slope[c] * rates[c]).astype(BF16) for c in each]
    ones = jnp.ones((TILE, TILE), BF16)
    for c in each:
        new = w1[c] - dot(scaled_inner[c], wide[c], NT)
        w1[c] = new
        w1b[c] = split_bias(new)
    for c in each:
        new = w2t[c] - dot(scaled_outer[c], hidden[c], NT)
        w2t[c] = new
        w2tb[c] = new.astype(BF16)
        bias2[c] = bias2[c] - dot(scaled_outer[c], ones, NT)
        new = w2[c] - dot(hidden[c], scaled_outer[c], NT)
        w2[c] = new
        w2b[c] = new.astype(BF16)
    return answer


def flipped(index, bits, count):
    result = 0
    place = 1
    while place < count:
        bit = lax.rem(index // place, 2)
        result = result + place * ((1 - bit) if (bits // place) % 2 else bit)
        place *= 2
    return result


def partner(index, step, count):
    if count & (count - 1) == 0:
        return flipped(index, step, count)
    return lax.rem(index + step, count)


def greet(axes):
    barrier = pltpu.get_barrier_semaphore()
    for axis, count in axes:
        me = lax.axis_index(axis)
        for step in range(1, count):
            pl.semaphore_signal(
                barrier,
                inc=1,
                device_id={axis: lax.rem(me + step, count)},
                device_id_type=MESH,
            )
    pl.semaphore_wait(barrier, sum(count - 1 for _, count in axes))


def block_of(heads):
    return max(n for n in (4, 3, 2, 1) if heads % n == 0)


def project(sizes, group_me, mine, qkv, rate_weight, base, load, load_rates, weights, sums,
            land, weight_sem, token_send, token_recv, between, ready):
    places, group, seqs, heads, parts, count, own, pieces = sizes
    piece = mine.shape[2] // pieces
    total = seqs * heads
    block = group * own
    several = block_of(heads)

    def span(cut):
        return slice(cut * piece, (cut + 1) * piece)

    def fetch(cut):
        return pltpu.make_async_copy(
            qkv.at[:, span(cut)], weights.at[cut], weight_sem.at[cut]
        )

    def move(n, cut, step, peer, source):
        return pltpu.make_async_remote_copy(
            src_ref=mine.at[n, :, span(cut)],
            dst_ref=land.at[n, cut, source],
            send_sem=token_send.at[n, cut, step],
            recv_sem=token_recv.at[n, cut, source],
            device_id={"tensor": peer},
            device_id_type=MESH,
        )

    for n in range(seqs):
        for cut in range(pieces):
            for step in range(group - 1, 0, -1):
                move(n, cut, step, partner(group_me, step, group), group_me).start()
    for cut in range(pieces):
        fetch(cut).start()
    if places * count > total:
        load[...] = jnp.zeros_like(load)
    between()
    gates = []
    for n in range(seqs):
        logit = None
        for cut in range(pieces):
            land[n, cut, group_me] = mine[n, :, span(cut)]
            if n == 0:
                fetch(cut).wait()
            for step in range(group - 1, 0, -1):
                peer = partner(group_me, step, group)
                move(n, cut, step, peer, peer).wait_recv()
            tokens = land[n, cut].astype(F32).reshape(block, piece).astype(BF16)
            more = dot(rate_weight[:, span(cut)], tokens, NT)
            logit = more if logit is None else logit + more

            def some_heads(index, carry):
                start = pl.multiple_of(index * (several * 3 * HEAD), 64)
                rows = pl.ds(start, several * 3 * HEAD)
                part = dot(weights[cut, rows, :], tokens, NT)
                part = part.reshape(several, 3 * HEAD, block)
                at = pl.ds(index * several, several)
                sums[at] = part if cut == 0 else sums[at] + part
                return carry

            lax.fori_loop(0, heads // several, some_heads, 0)
        gates.append(jax.nn.sigmoid(logit))
        for head in range(heads):
            place, c = divmod(head * seqs + n, count)
            for part in range(parts):
                load[place, c, part] = sums[head, :, part * TILE : (part + 1) * TILE].astype(BF16)
        if n + 1 < seqs:
            ready(n)
    for place in range(places):
        for part in range(parts):
            coarse, fine = [], []
            for c in range(count):
                head, n = divmod(min(place * count + c, total - 1), seqs)
                row = base[head] * gates[n][head : head + 1, part * TILE : (part + 1) * TILE]
                short = row.astype(BF16).astype(F32)
                coarse.append(short)
                fine.append(row - short)
            fill = [jnp.zeros((PAIRS - count, TILE), F32)] if count < PAIRS else []
            load_rates[place, part] = jnp.concatenate(
                coarse + fill + fine + fill, axis=0
            ).astype(BF16)
    ready(seqs - 1)

    def drain():
        for n in range(seqs):
            for cut in range(pieces):
                for step in range(group - 1, 0, -1):
                    move(n, cut, step, partner(group_me, step, group), group_me).wait_send()

    return drain


def layer_kernel(sizes, mine, qkv, rate_weight, base, first_w, first_b, second_w, second_b,
                 norm_gain, norm_shift, mix_weight, out,
                 w1, w2, w2t, w1b, w2b, w2tb, bias2, low, gain, shift,
                 x, x_rates, arrive, arrive_rates, outs, back, weights, sums, land, mix, ready, shares,
                 weight_sem, token_send, token_recv, mix_sem,
                 send_sem, recv_sem, own_sem, back_send, back_recv, back_own,
                 share_send, share_recv):
    places, group, seqs, heads, parts, count, own_rows, pieces = sizes
    total_chains = seqs * heads
    me = lax.axis_index("seq")
    group_me = lax.axis_index("tensor")
    greet((("tensor", group), ("seq", places)))

    def forward(step, c, peer, source):
        return pltpu.make_async_remote_copy(
            src_ref=x.at[peer, c],
            dst_ref=arrive.at[source, c],
            send_sem=send_sem.at[step, c],
            recv_sem=recv_sem.at[source, c],
            device_id={"seq": peer},
            device_id_type=MESH,
        )

    def forward_rates(step, peer, source):
        return pltpu.make_async_remote_copy(
            src_ref=x_rates.at[peer],
            dst_ref=arrive_rates.at[source],
            send_sem=send_sem.at[step, count],
            recv_sem=recv_sem.at[source, count],
            device_id={"seq": peer},
            device_id_type=MESH,
        )

    def homeward(place, source):
        return pltpu.make_async_remote_copy(
            src_ref=outs.at[place],
            dst_ref=back.at[source],
            send_sem=back_send.at[place],
            recv_sem=back_recv.at[source],
            device_id={"seq": place},
            device_id_type=MESH,
        )

    own = pltpu.make_async_copy(x.at[me], arrive.at[me], own_sem.at[0])
    own_rates = pltpu.make_async_copy(x_rates.at[me], arrive_rates.at[me], own_sem.at[1])
    own_back = pltpu.make_async_copy(outs.at[me], back.at[me], back_own)
    mix_copy = pltpu.make_async_copy(mix_weight, mix, mix_sem)
    state = (w1, w2, w2t, w1b, w2b, w2tb)
    consts = (gain, shift)
    params = (first_w, first_b, second_w, second_b, norm_gain, norm_shift)

    def between():
        mix_copy.start()
        load_state(me, count, total_chains, params, consts, state, bias2)
        low[...] = jnp.zeros_like(low)

    def ready_rows(n):
        if n == seqs - 1:
            for step in range(places - 1, 0, -1):
                forward_rates(step, partner(me, step, places), me).start()
            own.start()
            own_rates.start()
        for step in range(places - 1, 0, -1):
            peer = partner(me, step, places)
            for c in range(count):

                @pl.when(lax.rem(peer * count + c, seqs) == n)
                def _():
                    forward(step, c, peer, me).start()

    drain = project(
        sizes, group_me, mine, qkv, rate_weight, base, x, x_rates, weights, sums, land,
        weight_sem, token_send, token_recv, between, ready_rows,
    )
    lane = lax.broadcasted_iota(jnp.int32, (HEAD, TILE), 1)

    def finish(place, part, answer):
        for c in range(count):
            outs[place, part, c * HEAD : (c + 1) * HEAD, :] = jnp.where(
                lane < MB, low[c], answer[c]
            ).astype(BF16)

    def send_home(place):
        @pl.when(place == me)
        def _():
            own_back.start()

        @pl.when(place != me)
        def _():
            homeward(place, me).start()

    def body(place, carry):
        @pl.when(place == me)
        def _():
            own.wait()
            own_rates.wait()

        @pl.when(place != me)
        def _():
            forward_rates(0, place, place).wait_recv()
            for c in range(count):
                forward(0, c, place, place).wait_recv()

        for part in range(parts):
            tile = (arrive.at[place], arrive_rates.at[place], part)
            if part:
                old_place, old_part = place, part - 1
            else:
                old_place, old_part = jnp.maximum(place - 1, 0), parts - 1
            before = (arrive.at[old_place], None, old_part)
            answer = mini_batch(count, True, True, tile, before, consts, state, bias2)
            finish(old_place, old_part, answer)
            if not part:

                @pl.when(place > 0)
                def _():
                    send_home(place - 1)

            answer = mini_batch(count, False, True, tile, tile, consts, state, bias2)
            for c in range(count):
                low[c] = answer[c]
        return carry

    lax.fori_loop(0, places, body, 0)
    last = (arrive.at[places - 1], None, parts - 1)
    answer = mini_batch(count, True, False, last, last, consts, state, bias2)
    finish(places - 1, parts - 1, answer)
    send_home(places - 1)
    own_back.wait()
    for step in range(1, places):
        peer = partner(me, step, places)
        forward_rates(step, peer, me).wait_send()
        for c in range(count):
            forward(step, c, peer, me).wait_send()
        homeward(peer, peer).wait_recv()
        homeward(peer, me).wait_send()


    mix_copy.wait()

    def heads_of(n):
        tiles = []
        for part in range(parts):
            found = []
            for head in range(heads):
                place, c = divmod(head * seqs + n, count)
                found.append(back[place, part, c * HEAD : (c + 1) * HEAD, :].astype(F32))
            tiles.append(jnp.concatenate(found, axis=0).T)
        return jnp.concatenate(tiles, axis=0).astype(BF16)

    rows = [heads_of(n) for n in range(seqs)]
    width = mix.shape[1]
    cuts = ready.shape[0]
    piece = width // cuts

    def move(cut, row, slot, step):
        peer = partner(group_me, step, group)
        return pltpu.make_async_remote_copy(
            src_ref=ready.at[cut, partner(group_me, row, group)],
            dst_ref=shares.at[cut, slot],
            send_sem=share_send.at[cut, slot],
            recv_sem=share_recv.at[cut, slot],
            device_id={"tensor": peer},
            device_id_type=MESH,
        )

    def sends(cut):
        if group != 4:
            return [(step, step, step) for step in range(group - 1, 0, -1)], None
        near, far = ((1, 2), (2, 1))[cut % 2]
        return [(3, 3, near), (near, near, near)], (far, far, far)

    def pass_on(cut):
        first, later = sends(cut)
        if later is None:
            return
        move(cut, *first[0]).wait_recv()
        row = partner(group_me, later[0], group)
        joint = ready[cut, row].astype(F32) + shares[cut, 3].astype(F32)
        ready[cut, row] = joint.astype(BF16)
        move(cut, *later).start()

    both = jnp.concatenate(rows, axis=0)
    for cut in range(cuts):
        part = dot(both, mix[:, cut * piece : (cut + 1) * piece])
        part = part.reshape(seqs, group, own_rows, piece)
        ready[cut] = jnp.concatenate([part[n] for n in range(seqs)], axis=1).astype(BF16)
        for each in sends(cut)[0]:
            move(cut, *each).start()
        if cut >= 2:
            pass_on(cut - 2)
    for cut in range(cuts - 2, cuts):
        pass_on(cut)
    for cut in range(cuts):
        result = ready[cut, group_me].astype(F32)
        first, later = sends(cut)
        ends = first if later is None else [first[1], later]
        for each in ends:
            move(cut, *each).wait_recv()
            result = result + shares[cut, each[1]].astype(F32)
        out[:, cut * piece : (cut + 1) * piece] = result.astype(BF16)
    for cut in range(cuts):
        first, later = sends(cut)
        for each in first + ([] if later is None else [later]):
            move(cut, *each).wait_send()
    drain()


def shards(
    tokens,
    qkv_weight,
    rate_weight,
    base_rate,
    first_w,
    first_b,
    second_w,
    second_b,
    norm_gain,
    norm_shift,
    out_weight,
):
    places = lax.axis_size("seq")
    group = lax.axis_size("tensor")
    seqs, own, width = tokens.shape
    block = own * group
    heads, _, inner = first_w.shape
    assert block % TILE == 0
    parts = block // TILE
    count = -(-seqs * heads // places)
    assert count <= PAIRS
    pieces = cuts = 6
    piece = width // pieces
    sizes = (places, group, seqs, heads, parts, count, own, pieces)
    vmem = pl.BlockSpec(memory_space=pltpu.VMEM)
    whole = pl.BlockSpec(memory_space=pl.ANY)
    dma = pltpu.SemaphoreType.DMA
    out = pl.pallas_call(
        functools.partial(layer_kernel, sizes),
        out_shape=jax.ShapeDtypeStruct((seqs * own, width), BF16),
        in_specs=[vmem, whole, vmem, pl.BlockSpec(memory_space=pltpu.SMEM)] + [vmem] * 6 + [whole],
        out_specs=vmem,
        scratch_shapes=[
            pltpu.VMEM((count, inner, TILE), F32),
            pltpu.VMEM((count, inner, HEAD), F32),
            pltpu.VMEM((count, HEAD, inner), F32),
            pltpu.VMEM((count, inner, TILE), BF16),
            pltpu.VMEM((count, inner, HEAD), BF16),
            pltpu.VMEM((count, HEAD, inner), BF16),
            pltpu.VMEM((count, HEAD, TILE), F32),
            pltpu.VMEM((count, HEAD, TILE), F32),
            pltpu.VMEM((count, HEAD, TILE), F32),
            pltpu.VMEM((count, HEAD, TILE), F32),
            pltpu.VMEM((places, count, parts, 3 * HEAD, TILE), BF16),
            pltpu.VMEM((places, parts, 2 * PAIRS, TILE), BF16),
            pltpu.VMEM((places, count, parts, 3 * HEAD, TILE), BF16),
            pltpu.VMEM((places, parts, 2 * PAIRS, TILE), BF16),
            pltpu.VMEM((places, parts, count * HEAD, TILE), BF16),
            pltpu.VMEM((places, parts, count * HEAD, TILE), BF16),
            pltpu.VMEM((pieces, heads * 3 * HEAD, piece), BF16),
            pltpu.VMEM((heads, 3 * HEAD, block), F32),
            pltpu.VMEM((seqs, pieces, group, own, piece), BF16),
            pltpu.VMEM((heads * HEAD, width), BF16),
            pltpu.VMEM((cuts, group, seqs * own, width // cuts), BF16),
            pltpu.VMEM((cuts, group, seqs * own, width // cuts), BF16),
            dma((pieces,)),
            dma((seqs, pieces, group)),
            dma((seqs, pieces, group)),
            dma,
            dma((places, count + 1)),
            dma((places, count + 1)),
            dma((2,)),
            dma((places,)),
            dma((places,)),
            dma,
            dma((cuts, group)),
            dma((cuts, group)),
        ],
        compiler_params=pltpu.CompilerParams(
            collective_id=1, has_side_effects=True, vmem_limit_bytes=56 * 1024 * 1024
        ),
    )(
        tokens,
        qkv_weight.reshape(-1, width),
        rate_weight,
        base_rate,
        first_w,
        first_b,
        jnp.swapaxes(second_w, 1, 2),
        second_b,
        norm_gain,
        norm_shift,
        out_weight,
    )
    return out.reshape(tokens.shape)


def solution(mesh):
    in_specs = (
        P(None, ("seq", "tensor"), None),
        P("tensor", None, None),
        P("tensor", None),
        P("tensor"),
        P("tensor", None, None),
        P("tensor", None),
        P("tensor", None, None),
        P("tensor", None),
        P("tensor", None),
        P("tensor", None),
        P("tensor", None),
    )
    out_specs = P(None, ("seq", "tensor"), None)
    return jax.shard_map(shards, mesh=mesh, in_specs=in_specs, out_specs=out_specs, check_vma=False)
```
